32 devices in a mesh: grp: 2 (over x), tm: 8 (over z, y), head: 2 (over core).
Axes of the slice: x: 2, y: 2, z: 4, core: 2. Of those that a mesh axis runs over, the one named last changes fastest.
Arguments:
- queries: bfloat16 [2048, 6144], P(('grp', 'tm'), 'head'), parts along dimension 0, may hold values from -130 to 130
- keys: bfloat16 [2048, 1024], P(('grp', 'tm'), 'head'), parts along dimension 0, may hold values from -7 to 7
- values: bfloat16 [2048, 1024], P(('grp', 'tm'), 'head'), parts along dimension 0, may hold values from -6 to 6
- span_mask: int32 [8, 4], P('grp'), parts along dimension 0, may hold values from 0 to 1, as said below
- section: int32 [8], P('grp'), parts along dimension 0, may hold values from 0 to 3
- section_gate: float32 [4, 6144], P(None, 'head'), may hold values from 0.1 to 1.9
Outputs:
- mixed: bfloat16 [2048, 6144], P(('grp', 'tm'), 'head'), parts along dimension 0
- log_total: float32 [48, 2048], P('head', ('grp', 'tm')), parts along dimension 1
The draws below stay inside these ranges and needn't reach their ends.
There are 2 independent parts, one for each index of `grp`. The reference program is written for one: setup_inputs(seed, part) draws one part's arguments, and reference() takes and returns one part's arrays. A program takes and returns all parts, laid end to end along the dimension named above; an argument that names none is the same for every part. Nothing has to cross between parts.
Inputs may be any that keep to these rules, and one draw needn't show every extreme that they name: `span_mask`: the first column and the diagonal are 1 and everything above the diagonal is 0.
All inputs are finite; a program needn't handle non-finite values.
Results may differ from the reference program's by a relative error of at most 0.006.
Values may be sent and summed in bfloat16 or wider, within the bound.
No kernel may reach another device: no remote copies, remote signals or barrier semaphores. Data moves between devices by JAX's collectives and lax.ppermute only.
A program may use at most 64 MiB of HBM per device.

```python
import math
import jax
import jax.numpy as jnp
from jax import lax

QUERY_HEADS = 48
KEY_VALUE_HEADS = 8
HEAD_SIZE = 128
CH = 256
SECTIONS = 4
CLIP_TOKENS = 1024
NC = 4


def paired_fields(key):
    base = jax.random.fold_in(key, 7)
    random_key_first, key_b = jax.random.split(base, 2)
    keys_float = jnp.clip(jax.random.normal(random_key_first, (CLIP_TOKENS, KEY_VALUE_HEADS * HEAD_SIZE), jnp.float32), -6.0, 6.0)
    queries_f = 2.0 * jnp.clip(jax.random.normal(key_b, (CLIP_TOKENS, QUERY_HEADS * HEAD_SIZE), jnp.float32), -6.0, 6.0)
    return (queries_f, keys_float)


def draw_queries(key, part):
    return paired_fields(key)[0].astype(jnp.bfloat16)


def draw_keys(key, part):
    return paired_fields(key)[1].astype(jnp.bfloat16)


def draw_span_mask(key, part):
    coin = jax.random.randint(jax.random.fold_in(key, 11), (NC, NC), 0, 2)
    row_ids = jnp.arange(NC, dtype=jnp.int32)[:, None]
    col_ids = jnp.arange(NC, dtype=jnp.int32)[None, :]
    result = jnp.where(col_ids < row_ids, coin, 0)
    result = jnp.where(col_ids == row_ids, 1, result)
    result = jnp.where(col_ids == 0, 1, result)
    return result.astype(jnp.int32)


def touch_ends(drawn, stream_key, low, largest):
    dims = drawn.shape
    place = [jax.random.randint(jax.random.fold_in(stream_key, axis), (), 0, dims[axis]) for axis in range(len(dims))]
    drawn = drawn.at[tuple(place)].set(low)
    longest = dims.index(max(dims))
    place[longest] = (place[longest] + 1) % dims[longest]
    return drawn.at[tuple(place)].set(largest)


def block_scale(own_key, shape, shards, least, high):
    factor_of, own = 1.0, jax.random.fold_in(own_key, 6)
    for axis_at, parts in shards:
        heights = jnp.exp(jax.random.uniform(jax.random.fold_in(own, axis_at), (parts,), jnp.float32, least / len(shards), high / len(shards)))
        factor_of = factor_of * jnp.repeat(heights, shape[axis_at] // parts).reshape([-1 if axis == axis_at else 1 for axis in range(len(shape))])
    return factor_of


def scatter_about(stream_key, dims, deviation, most, shards=(), held_as=jnp.bfloat16):
    entries = deviation * jax.random.normal(stream_key, dims, jnp.float32)
    if shards:
        entries = entries * block_scale(stream_key, dims, shards, -0.22, 0.18)
    return jnp.clip(entries, -most, most).astype(held_as)


def setup_inputs(seed: int = 0, part: int = 0) -> dict:
    arg_keys = jax.random.split(jax.random.key(seed), 7)
    own_keys = jax.random.split(jax.random.fold_in(arg_keys[6], part), 7)
    queries = draw_queries(jax.random.fold_in(jax.random.fold_in(arg_keys[6], part), 71), part)
    keys = draw_keys(jax.random.fold_in(jax.random.fold_in(arg_keys[6], part), 71), part)
    values = scatter_about(own_keys[2], (CLIP_TOKENS, KEY_VALUE_HEADS * HEAD_SIZE), 1.0, 6.0, ((0, 8), (1, 2)))
    span_mask = draw_span_mask(jax.random.fold_in(jax.random.fold_in(arg_keys[6], part), 71), part)
    section = touch_ends(jax.random.randint(own_keys[4], (NC,), 0, SECTIONS), jax.random.fold_in(own_keys[4], 1), 0, SECTIONS - 1).astype(jnp.int32)
    section_gate = jnp.clip(1.0 + 0.18 * jax.random.normal(arg_keys[5], (SECTIONS, QUERY_HEADS * HEAD_SIZE), jnp.float32), 0.1, 1.9)
    return dict(queries=queries, keys=keys, values=values, span_mask=span_mask, section=section, section_gate=section_gate)


def reference(queries, keys, values, span_mask, section, section_gate):
    total_rows = queries.shape[0]
    query_group = QUERY_HEADS // KEY_VALUE_HEADS
    span_ids = (jnp.arange(total_rows, dtype=jnp.int32) // CH).astype(jnp.int32)
    allowed = jnp.take(jnp.take(span_mask, span_ids, axis=0), span_ids, axis=1) > 0
    scale = 1.0 / math.sqrt(HEAD_SIZE)

    def one_head(head_index):
        start_q = (head_index * HEAD_SIZE).astype(jnp.int32)
        start_k = (head_index // query_group * HEAD_SIZE).astype(jnp.int32)
        query_head = lax.dynamic_slice_in_dim(queries, start_q, HEAD_SIZE, 1)
        key_head = lax.dynamic_slice_in_dim(keys, start_k, HEAD_SIZE, 1)
        value_head = lax.dynamic_slice_in_dim(values, start_k, HEAD_SIZE, 1)
        score = jnp.dot(query_head, key_head.T, preferred_element_type=jnp.float32) * scale
        score = jnp.where(allowed, score, -1e+30)
        top = lax.optimization_barrier(jnp.max(score, axis=1))
        weight = jnp.where(allowed, jnp.exp(score - top[:, None]), 0.0)
        total = lax.optimization_barrier(jnp.sum(weight, axis=1))
        attended = jnp.dot(weight.astype(jnp.bfloat16), value_head, preferred_element_type=jnp.float32) / total[:, None]
        return (attended, top + jnp.log(total))
    attended, log_total = lax.map(one_head, jnp.arange(QUERY_HEADS, dtype=jnp.int32))
    attended = jnp.transpose(attended, (1, 0, 2)).reshape(total_rows, QUERY_HEADS * HEAD_SIZE)
    gate_rows = jnp.take(section_gate, jnp.take(section, span_ids), axis=0)
    mixed = (gate_rows * attended).astype(jnp.bfloat16)
    return (mixed, log_total)
```

```python
import functools
import math

import jax
import jax.numpy as jnp
from jax import lax
from jax.experimental import pallas as pl
from jax.experimental.pallas import tpu as pltpu
from jax.sharding import PartitionSpec as P

HEAD_SIZE = 128
CH = 256
LOG2E = math.log2(math.e)
LN2 = math.log(2.0)


def attend_kernel(items, per_span, first, last, refs_in, refs_out):
    refs = list(refs_in)
    mask_ref, section_ref, q_ref = refs[:3]
    refs = refs[3:]
    if last:
        gate_ref = refs.pop(0)
    if not first:
        acc_in, stat_in = refs.pop(0), refs.pop(0)
    key_refs, value_refs = refs[: len(items)], refs[len(items) :]
    if last:
        mixed_ref, log_ref, acc, stat = refs_out
    else:
        acc, stat = refs_out
    rows = q_ref.shape[0]
    kv_heads = acc.shape[0]
    group = q_ref.shape[1] // HEAD_SIZE // kv_heads
    span = lax.axis_index("tm") // per_span
    scale = LOG2E / math.sqrt(HEAD_SIZE)

    if first:
        for h in range(kv_heads):
            stat[h, 0:1, :] = jnp.full((1, group * rows), -1e30, jnp.float32)
            stat[h, 1:2, :] = jnp.zeros((1, group * rows), jnp.float32)
            acc[h] = jnp.zeros(acc.shape[1:], jnp.float32)
    else:
        for h in range(kv_heads):
            stat[h, 0:2, :] = stat_in[h, 0:2, :]
            acc[h] = acc_in[h]

    def visit(k_ref, v_ref):
        for h in range(kv_heads):
            queries = jnp.concatenate(
                [q_ref[:, (h * group + g) * HEAD_SIZE : (h * group + g + 1) * HEAD_SIZE] for g in range(group)], axis=0
            )
            k = k_ref[:, h * HEAD_SIZE : (h + 1) * HEAD_SIZE]
            v = v_ref[:, h * HEAD_SIZE : (h + 1) * HEAD_SIZE]
            score = scale * lax.dot_general(k, queries, (((1,), (1,)), ((), ())), preferred_element_type=jnp.float32)
            old = stat[h, 0:1, :]
            top = jnp.maximum(old, jnp.max(score, axis=0, keepdims=True))
            weight = jnp.exp2(score - top)
            factor = jnp.exp2(old - top)
            stat[h, 0:1, :] = top
            stat[h, 1:2, :] = stat[h, 1:2, :] * factor + jnp.sum(weight, axis=0, keepdims=True)
            part = lax.dot_general(
                v, weight.astype(jnp.bfloat16), (((0,), (0,)), ((), ())), preferred_element_type=jnp.float32
            )
            acc[h] = acc[h] * factor + part

    for distance, k_ref, v_ref in zip(items, key_refs, value_refs):
        if distance == 0:
            visit(k_ref, v_ref)
        else:
            behind = jnp.maximum(span - distance, 0)
            seen = jnp.logical_and(span >= distance, mask_ref[span, behind] > 0)
            pl.when(seen)(functools.partial(visit, k_ref, v_ref))

    if last:
        gate_row = gate_ref[pl.ds(section_ref[span], 1), :]
        for h in range(kv_heads):
            total = stat[h, 1:2, :]
            log_total = stat[h, 0:1, :] * LN2 + jnp.log(total)
            attended = acc[h] / total
            for g in range(group):
                head = h * group + g
                columns = slice(head * HEAD_SIZE, (head + 1) * HEAD_SIZE)
                block = attended[:, g * rows : (g + 1) * rows].T
                mixed_ref[:, columns] = (gate_row[:, columns] * block).astype(jnp.bfloat16)
                log_ref[head : head + 1, :] = log_total[:, g * rows : (g + 1) * rows]


def attend(name, items, per_span, state, last, mask, section, queries, gate, kv_heads):
    rows, width = queries.shape
    heads = width // HEAD_SIZE
    group = heads // kv_heads
    first = state is None
    operands = [mask, section, queries]
    specs = [pl.BlockSpec(memory_space=pltpu.SMEM)] * 2 + [pl.BlockSpec(memory_space=pltpu.VMEM)]
    if last:
        operands.append(gate)
    if not first:
        operands += list(state)
    operands += [k for _, k, _ in items] + [v for _, _, v in items]
    specs += [pl.BlockSpec(memory_space=pltpu.VMEM)] * (len(operands) - len(specs))
    acc_shape = (kv_heads, HEAD_SIZE, group * rows)
    stat_shape = (kv_heads, 8, group * rows)
    scratch = []
    if last:
        out_shape = (
            jax.ShapeDtypeStruct((rows, width), jnp.bfloat16),
            jax.ShapeDtypeStruct((heads, rows), jnp.float32),
        )
        scratch = [pltpu.VMEM(acc_shape, jnp.float32), pltpu.VMEM(stat_shape, jnp.float32)]
    else:
        out_shape = (
            jax.ShapeDtypeStruct(acc_shape, jnp.float32),
            jax.ShapeDtypeStruct(stat_shape, jnp.float32),
        )
    count = len(operands)

    def kernel(*refs):
        attend_kernel([d for d, _, _ in items], per_span, first, last, refs[:count], refs[count:])

    keys_seen = len(items) * rows
    return pl.pallas_call(
        kernel,
        out_shape=out_shape,
        in_specs=specs,
        out_specs=(pl.BlockSpec(memory_space=pltpu.VMEM),) * 2,
        scratch_shapes=scratch,
        compiler_params=pltpu.CompilerParams(vmem_limit_bytes=24 * 1024 * 1024),
        cost_estimate=pl.CostEstimate(
            flops=8 * keys_seen * rows * width,
            bytes_accessed=rows * width * 8,
            transcendentals=keys_seen * rows * heads,
        ),
        name=name,
    )(*operands)


def on_device(queries, keys, values, span_mask, section, section_gate):
    rows = queries.shape[0]
    kv_heads = keys.shape[1] // HEAD_SIZE
    count = lax.axis_size("tm")
    per_span = CH // rows
    spans = count // per_span

    def onward(value, distance):
        pairs = [(i, i + per_span) for i in range((distance - 1) * per_span, count - per_span)]
        return lax.ppermute(value, "tm", pairs)

    def around(value, distance, turn):
        pairs = [
            (s * per_span + i, s * per_span + (i + turn) % per_span)
            for s in range(distance, spans)
            for i in range(per_span)
        ]
        return lax.ppermute(value, "tm", pairs)

    blocks = []
    held = (keys, values)
    for distance in range(spans):
        if distance:
            held = tuple(onward(x, distance) for x in held)
        blocks.append((distance, 0, held))
        for turn in range(1, per_span):
            blocks.append((distance, turn, tuple(around(x, distance, turn) for x in held)))
    blocks.sort(key=lambda b: (b[0] + (b[1] > 0), -b[1]))
    blocks = [(d, k, v) for d, _, (k, v) in blocks]
    groups = [blocks[i : i + 3] for i in range(0, len(blocks) - 1, 3)]
    groups[-1] = [b for b in groups[-1] if b is not blocks[-1]]
    groups.append([blocks[-1]])
    groups = [g for g in groups if g]
    state = None
    for at, group in enumerate(groups):
        state = attend(
            "attend_%d" % at, group, per_span, state, at == len(groups) - 1,
            span_mask, section, queries, section_gate, kv_heads,
        )
    return state


def solution(mesh):
    placed = (
        P(("grp", "tm"), "head"),
        P(("grp", "tm"), "head"),
        P(("grp", "tm"), "head"),
        P("grp", None),
        P("grp"),
        P(None, "head"),
    )
    return jax.shard_map(
        on_device,
        mesh=mesh,
        in_specs=placed,
        out_specs=(P(("grp", "tm"), "head"), P("head", ("grp", "tm"))),
        check_vma=False,
    )
```

```python
import math

import jax
import jax.numpy as jnp
from jax import lax
from jax.experimental import pallas as pl
from jax.experimental.pallas import tpu as pltpu
from jax.sharding import PartitionSpec as P

HEAD_SIZE = 128
CH = 256
LOG2E = math.log2(math.e)
LN2 = math.log(2.0)
FAR = 1e30


def attend_kernel(distances, per_span, first, last, refs_in, refs_out):
    refs = list(refs_in)
    mask_ref, section_ref, q_ref = refs[:3]
    refs = refs[3:]
    if last:
        gate_ref = refs.pop(0)
    if not first:
        acc_in, stat_in = refs.pop(0), refs.pop(0)
    blocks = len(distances)
    key_refs, value_refs = refs[:blocks], refs[blocks:]
    if last:
        mixed_ref, log_ref = refs_out
    else:
        acc_out, stat_out = refs_out
    rows, heads = q_ref.shape[0], q_ref.shape[1] // HEAD_SIZE
    kv_heads = key_refs[0].shape[1] // HEAD_SIZE
    group = heads // kv_heads
    span = lax.axis_index("tm") // per_span
    scale = LOG2E / math.sqrt(HEAD_SIZE)
    seen = []
    for distance in distances:
        if distance == 0:
            seen.append(None)
        else:
            behind = jnp.maximum(span - distance, 0)
            seen.append(jnp.logical_and(span >= distance, mask_ref[span, behind] > 0))
    if last:
        gate_row = gate_ref[pl.ds(section_ref[span], 1), :]

    for h in range(kv_heads):
        inside = slice(h * HEAD_SIZE, (h + 1) * HEAD_SIZE)
        queries = jnp.concatenate(
            [q_ref[:, (h * group + g) * HEAD_SIZE : (h * group + g + 1) * HEAD_SIZE] for g in range(group)], axis=0
        )
        scores = [
            scale * lax.dot_general(k[:, inside], queries, (((1,), (1,)), ((), ())), preferred_element_type=jnp.float32)
            for k in key_refs
        ]
        old = None if first else stat_in[h, 0:1, :]
        top = old
        for score, see in zip(scores, seen):
            row = jnp.max(score, axis=0, keepdims=True)
            if see is not None:
                row = jnp.where(see, row, -FAR)
            top = row if top is None else jnp.maximum(top, row)
        weights = [
            jnp.exp2(score - (top if see is None else jnp.where(see, top, FAR))) for score, see in zip(scores, seen)
        ]
        total = sum(jnp.sum(weight, axis=0, keepdims=True) for weight in weights)
        attended = lax.dot_general(
            jnp.concatenate([v[:, inside] for v in value_refs], axis=0),
            jnp.concatenate([weight.astype(jnp.bfloat16) for weight in weights], axis=0),
            (((0,), (0,)), ((), ())),
            preferred_element_type=jnp.float32,
        )
        if not first:
            factor = jnp.exp2(old - top)
            total += stat_in[h, 1:2, :] * factor
            attended += acc_in[h] * factor
        if not last:
            stat_out[h, 0:1, :] = top
            stat_out[h, 1:2, :] = total
            acc_out[h] = attended
            continue
        log_total = top * LN2 + jnp.log(total)
        attended = attended * (1.0 / total)
        for g in range(group):
            head = h * group + g
            columns = slice(head * HEAD_SIZE, (head + 1) * HEAD_SIZE)
            block = attended[:, g * rows : (g + 1) * rows].T
            mixed_ref[:, columns] = (gate_row[:, columns] * block).astype(jnp.bfloat16)
            log_ref[head : head + 1, :] = log_total[:, g * rows : (g + 1) * rows]


def attend(name, blocks, per_span, state, last, mask, section, queries, gate):
    rows, width = queries.shape
    heads = width // HEAD_SIZE
    kv_heads = blocks[0][1].shape[1] // HEAD_SIZE
    group = heads // kv_heads
    first = state is None
    operands = [mask, section, queries]
    specs = [pl.BlockSpec(memory_space=pltpu.SMEM)] * 2
    if last:
        operands.append(gate)
    if not first:
        operands += list(state)
    operands += [k for _, k, _ in blocks] + [v for _, _, v in blocks]
    specs += [pl.BlockSpec(memory_space=pltpu.VMEM)] * (len(operands) - len(specs))
    if last:
        out_shape = (
            jax.ShapeDtypeStruct((rows, width), jnp.bfloat16),
            jax.ShapeDtypeStruct((heads, rows), jnp.float32),
        )
    else:
        out_shape = (
            jax.ShapeDtypeStruct((kv_heads, HEAD_SIZE, group * rows), jnp.float32),
            jax.ShapeDtypeStruct((kv_heads, 8, group * rows), jnp.float32),
        )
    count = len(operands)

    def kernel(*refs):
        attend_kernel([d for d, _, _ in blocks], per_span, first, last, refs[:count], refs[count:])

    keys_seen = len(blocks) * rows
    return pl.pallas_call(
        kernel,
        out_shape=out_shape,
        in_specs=specs,
        out_specs=(pl.BlockSpec(memory_space=pltpu.VMEM),) * 2,
        compiler_params=pltpu.CompilerParams(vmem_limit_bytes=24 * 1024 * 1024),
        cost_estimate=pl.CostEstimate(
            flops=8 * keys_seen * rows * width,
            bytes_accessed=rows * width * 8,
            transcendentals=keys_seen * rows * heads,
        ),
        name=name,
    )(*operands)


def on_device(queries, keys, values, span_mask, section, section_gate):
    rows = queries.shape[0]
    count = lax.axis_size("tm")
    per_span = CH // rows
    spans = count // per_span

    def onward(value):
        return lax.ppermute(value, "tm", [(i, (i + per_span) % count) for i in range(count)])

    def around(value, turn):
        pairs = [(i, i - i % per_span + (i + turn) % per_span) for i in range(count)]
        return lax.ppermute(value, "tm", pairs)

    held = (keys, values)
    waiting = [(0, keys, values)]
    state = None
    for distance in range(spans + 1):
        coming = []
        if distance < spans:
            for turn in range(1, per_span):
                coming.append((distance,) + tuple(around(x, turn) for x in held))
        if distance + 1 < spans:
            held = tuple(onward(x) for x in held)
            coming.append((distance + 1,) + held)
        last = distance == spans
        state = attend(
            "attend_%d" % distance, waiting, per_span, state, last, span_mask, section, queries, section_gate
        )
        if not last:
            held, state = lax.optimization_barrier((held, state))
            if distance + 1 < spans:
                coming[-1] = (distance + 1,) + held
        waiting = coming
    return state


def solution(mesh):
    placed = (
        P(("grp", "tm"), "head"),
        P(("grp", "tm"), "head"),
        P(("grp", "tm"), "head"),
        P("grp", None),
        P("grp"),
        P(None, "head"),
    )
    return jax.shard_map(
        on_device,
        mesh=mesh,
        in_specs=placed,
        out_specs=(P(("grp", "tm"), "head"), P("head", ("grp", "tm"))),
        check_vma=False,
    )
```

```python
import math

import jax
import jax.numpy as jnp
from jax import lax
from jax.experimental import pallas as pl
from jax.experimental.pallas import tpu as pltpu
from jax.sharding import PartitionSpec as P

HEAD_SIZE = 128
CH = 256
LOG2E = math.log2(math.e)
LN2 = math.log(2.0)
FAR = 1e30


def weigh_kernel(per_span, mask_ref, q_ref, k_ref, weight_ref, inverse_ref, log_ref, score_ref):
    rows, heads = q_ref.shape[0], q_ref.shape[1] // HEAD_SIZE
    kv_heads = k_ref.shape[1] // HEAD_SIZE
    group = heads // kv_heads
    spans = k_ref.shape[0] // CH
    span = lax.axis_index("tm") // per_span
    scale = LOG2E / math.sqrt(HEAD_SIZE)
    seen = [jnp.logical_and(span >= s, mask_ref[span, s] > 0) for s in range(spans)]
    for h in range(kv_heads):
        inside = slice(h * HEAD_SIZE, (h + 1) * HEAD_SIZE)
        queries = jnp.concatenate(
            [q_ref[:, (h * group + g) * HEAD_SIZE : (h * group + g + 1) * HEAD_SIZE] for g in range(group)], axis=0
        )
        top = None
        for s in range(spans):
            score = scale * lax.dot_general(
                k_ref[s * CH : (s + 1) * CH, inside], queries, (((1,), (1,)), ((), ())),
                preferred_element_type=jnp.float32,
            )
            score_ref[h % 2, s] = score
            row = jnp.where(seen[s], jnp.max(score, axis=0, keepdims=True), -FAR)
            top = row if top is None else jnp.maximum(top, row)
        total = 0.0
        for s in range(spans):
            weight = jnp.exp2(score_ref[h % 2, s] - jnp.where(seen[s], top, FAR))
            total += jnp.sum(weight, axis=0, keepdims=True)
            weight_ref[h, s * CH : (s + 1) * CH, :] = weight.astype(jnp.bfloat16)
        inverse_ref[h, 0:1, :] = 1.0 / total
        log_total = top * LN2 + jnp.log(total)
        for g in range(group):
            log_ref[h * group + g : h * group + g + 1, :] = log_total[:, g * rows : (g + 1) * rows]


def mix_kernel(per_span, section_ref, weight_ref, inverse_ref, gate_ref, v_ref, mixed_ref):
    rows, heads = mixed_ref.shape[0], mixed_ref.shape[1] // HEAD_SIZE
    kv_heads = v_ref.shape[1] // HEAD_SIZE
    group = heads // kv_heads
    span = lax.axis_index("tm") // per_span
    gate_row = gate_ref[pl.ds(section_ref[span], 1), :]
    for h in range(kv_heads):
        attended = lax.dot_general(
            v_ref[:, h * HEAD_SIZE : (h + 1) * HEAD_SIZE], weight_ref[h], (((0,), (0,)), ((), ())),
            preferred_element_type=jnp.float32,
        )
        attended = attended * inverse_ref[h, 0:1, :]
        for g in range(group):
            columns = slice((h * group + g) * HEAD_SIZE, (h * group + g + 1) * HEAD_SIZE)
            block = attended[:, g * rows : (g + 1) * rows].T
            mixed_ref[:, columns] = (gate_row[:, columns] * block).astype(jnp.bfloat16)


def on_device(queries, keys, values, span_mask, section, section_gate):
    rows, width = queries.shape
    heads, kv_heads = width // HEAD_SIZE, keys.shape[1] // HEAD_SIZE
    group = heads // kv_heads
    per_span = CH // rows
    all_keys = lax.all_gather(keys, "tm", axis=0, tiled=True)
    all_values = lax.all_gather(values, "tm", axis=0, tiled=True)
    total = all_keys.shape[0]
    smem, vmem = pl.BlockSpec(memory_space=pltpu.SMEM), pl.BlockSpec(memory_space=pltpu.VMEM)
    params = pltpu.CompilerParams(vmem_limit_bytes=(24 if total <= 2048 else 56) * 1024 * 1024)
    score_bytes = total * group * rows * 4

    def weigh(*refs):
        weigh_kernel(per_span, *refs)

    def mix(*refs):
        mix_kernel(per_span, *refs)

    weight, inverse, log_total = pl.pallas_call(
        weigh,
        out_shape=(
            jax.ShapeDtypeStruct((kv_heads, total, group * rows), jnp.bfloat16),
            jax.ShapeDtypeStruct((kv_heads, 8, group * rows), jnp.float32),
            jax.ShapeDtypeStruct((heads, rows), jnp.float32),
        ),
        in_specs=[smem, vmem, vmem],
        out_specs=(vmem,) * 3,
        scratch_shapes=[pltpu.VMEM((2, total // CH, CH, group * rows), jnp.float32)],
        compiler_params=params,
        cost_estimate=pl.CostEstimate(
            flops=4 * total * rows * width, bytes_accessed=kv_heads * score_bytes // 2, transcendentals=kv_heads * score_bytes // 4
        ),
        name="weigh",
    )(span_mask, queries, all_keys)
    mixed = pl.pallas_call(
        mix,
        out_shape=jax.ShapeDtypeStruct((rows, width), jnp.bfloat16),
        in_specs=[smem] + [vmem] * 4,
        out_specs=vmem,
        compiler_params=params,
        cost_estimate=pl.CostEstimate(
            flops=4 * total * rows * width, bytes_accessed=kv_heads * score_bytes // 2, transcendentals=0
        ),
        name="mix",
    )(section, weight, inverse, section_gate, all_values)
    return mixed, log_total


def solution(mesh):
    placed = (
        P(("grp", "tm"), "head"),
        P(("grp", "tm"), "head"),
        P(("grp", "tm"), "head"),
        P("grp", None),
        P("grp"),
        P(None, "head"),
    )
    return jax.shard_map(
        on_device,
        mesh=mesh,
        in_specs=placed,
        out_specs=(P(("grp", "tm"), "head"), P("head", ("grp", "tm"))),
        check_vma=False,
    )
```

```python
import math

import jax
import jax.numpy as jnp
from jax import lax
from jax.experimental import pallas as pl
from jax.experimental.pallas import tpu as pltpu
from jax.sharding import PartitionSpec as P

HEAD_SIZE = 128
CH = 256
LOG2E = math.log2(math.e)
LN2 = math.log(2.0)
FAR = 1e30
SCALE = LOG2E / math.sqrt(HEAD_SIZE)
HBM = pl.BlockSpec(memory_space=pltpu.HBM)
VMEM = pl.BlockSpec(memory_space=pltpu.VMEM)


def head_columns(h):
    return slice(h * HEAD_SIZE, (h + 1) * HEAD_SIZE)


def scores_of(k, queries):
    return SCALE * lax.dot_general(k, queries, (((1,), (1,)), ((), ())), preferred_element_type=jnp.float32)


def times_values(v, weight):
    return lax.dot_general(v, weight, (((0,), (0,)), ((), ())), preferred_element_type=jnp.float32)


def own_kernel(q_hbm, k_hbm, v_hbm, stacked, acc, stat, q, k, v, sems):
    copies = [
        pltpu.make_async_copy(src, dst, sems.at[i])
        for i, (src, dst) in enumerate([(q_hbm, q), (k_hbm, k), (v_hbm, v)])
    ]
    for copy in copies:
        copy.start()
    for copy in copies:
        copy.wait()
    rows = q.shape[0]
    group = stacked.shape[1] // rows
    for h in range(stacked.shape[0]):
        for g in range(group):
            stacked[h, g * rows : (g + 1) * rows, :] = q[:, head_columns(h * group + g)]
    for h in range(stacked.shape[0]):
        score = scores_of(k[:, head_columns(h)], stacked[h])
        top = jnp.max(score, axis=0, keepdims=True)
        weight = jnp.exp2(score - top)
        stat[h, 0:1, :] = top
        stat[h, 1:2, :] = jnp.sum(weight, axis=0, keepdims=True)
        acc[h] = times_values(v[:, head_columns(h)], weight.astype(jnp.bfloat16))


def flag_kernel(per_span, mask, section, gate, seen, gate_row):
    span = lax.axis_index("tm") // per_span
    for distance in range(seen.shape[0]):
        allowed = jnp.logical_and(span >= distance, mask[span, jnp.maximum(span - distance, 0)] > 0)
        seen[distance : distance + 1, :] = jnp.full((1, seen.shape[1]), allowed.astype(jnp.int32), jnp.int32)
    gate_row[...] = gate[pl.ds(section[span], 1), :]


def weigh(h, distances, stacked, seen, stat, key_refs):
    scores = [scores_of(k[:, head_columns(h)], stacked[h]) for k in key_refs]
    flags = [seen[d : d + 1, :] > 0 for d in distances]
    old = stat[h, 0:1, :]
    top = old
    for score, flag in zip(scores, flags):
        top = jnp.maximum(top, jnp.where(flag, jnp.max(score, axis=0, keepdims=True), -FAR))
    weights = [jnp.exp2(score - jnp.where(flag, top, FAR)) for score, flag in zip(scores, flags)]
    factor = jnp.exp2(old - top)
    total = stat[h, 1:2, :] * factor
    for weight in weights:
        total += jnp.sum(weight, axis=0, keepdims=True)
    return weights, top, total, factor


def step_kernel(distances, stacked, seen, acc_in, stat_in, *refs):
    count = len(distances)
    key_refs, value_refs, (acc, stat) = refs[:count], refs[count : 2 * count], refs[2 * count :]
    for h in range(stacked.shape[0]):
        weights, top, total, factor = weigh(h, distances, stacked, seen, stat_in, key_refs)
        stat[h, 0:1, :] = top
        stat[h, 1:2, :] = total
        acc[h] = acc_in[h] * factor + times_values(
            jnp.concatenate([v[:, head_columns(h)] for v in value_refs], axis=0),
            jnp.concatenate([weight.astype(jnp.bfloat16) for weight in weights], axis=0),
        )


def close_kernel(distances, stacked, seen, gate_row, acc_in, stat_in, *refs):
    key_refs, (part, last_weight, log_ref) = refs[: len(distances)], refs[len(distances) :]
    rows = log_ref.shape[1]
    group = stacked.shape[1] // rows
    for h in range(stacked.shape[0]):
        weights, top, total, factor = weigh(h, distances, stacked, seen, stat_in, key_refs)
        inverse = 1.0 / total
        log_total = top * LN2 + jnp.log(total)
        turned = (acc_in[h] * (factor * inverse)).T
        for at, weight in enumerate(weights):
            last_weight[h, :, head_columns(at)] = (weight * inverse).T.astype(jnp.bfloat16)
        for g in range(group):
            head = h * group + g
            inside = slice(g * rows, (g + 1) * rows)
            part[h, inside, :] = turned[inside, :] * gate_row[:, head_columns(head)]
            log_ref[head : head + 1, :] = log_total[:, inside]


def mix_kernel(gate_row, part, last_weight, *refs):
    value_refs, (mixed_hbm, mixed, sems) = refs[:-3], refs[-3:]
    kv_heads, width = part.shape[0], part.shape[1]
    rows = mixed.shape[0]
    group = width // rows
    copies = []
    for h in range(kv_heads):
        values = jnp.concatenate([v[:, head_columns(h)] for v in value_refs], axis=0)
        rest = jnp.dot(last_weight[h], values, preferred_element_type=jnp.float32)
        for g in range(group):
            inside = slice(g * rows, (g + 1) * rows)
            columns = head_columns(h * group + g)
            mixed[:, columns] = (part[h, inside, :] + gate_row[:, columns] * rest[inside, :]).astype(jnp.bfloat16)
        columns = pl.ds(h * group * HEAD_SIZE, group * HEAD_SIZE)
        copies.append(pltpu.make_async_copy(mixed.at[:, columns], mixed_hbm.at[:, columns], sems.at[h]))
        copies[-1].start()
    for copy in copies:
        copy.wait()


def on_device(queries, keys, values, span_mask, section, section_gate):
    rows, wide = queries.shape
    heads, kv_heads = wide // HEAD_SIZE, keys.shape[1] // HEAD_SIZE
    width = heads // kv_heads * rows
    count = lax.axis_size("tm")
    per_span = CH // rows
    spans = count // per_span
    params = pltpu.CompilerParams(vmem_limit_bytes=24 * 1024 * 1024)
    acc_shape = jax.ShapeDtypeStruct((kv_heads, HEAD_SIZE, width), jnp.float32)
    stat_shape = jax.ShapeDtypeStruct((kv_heads, 8, width), jnp.float32)

    def cost(blocks):
        return pl.CostEstimate(
            flops=40 * blocks * rows * rows * wide, bytes_accessed=rows * wide * 8, transcendentals=blocks * rows * rows * heads
        )

    def onward(value, distance):
        first = (distance - 1) * per_span
        pairs = [(i, i) for i in range(first)] + [
            (i, i + per_span if i + per_span < count else first + i % per_span) for i in range(first, count)
        ]
        return lax.ppermute(value, "tm", pairs)

    def around(value, distance, turn):
        pairs = [
            (i, i - i % per_span + (i + turn) % per_span if i >= distance * per_span else i) for i in range(count)
        ]
        return lax.ppermute(value, "tm", pairs)

    def travel(held, distance):
        turned, onwards = [], []
        for x in held:
            if distance + 1 < spans:
                onwards.append(onward(x, distance + 1))
            turned.append([around(x, distance, turn) for turn in range(1, per_span)])
        return list(zip(*turned)), onwards

    turned, held = travel((keys, values), 0)
    stacked, acc, stat = pl.pallas_call(
        own_kernel,
        out_shape=(jax.ShapeDtypeStruct((kv_heads, width, HEAD_SIZE), jnp.bfloat16), acc_shape, stat_shape),
        in_specs=[HBM] * 3,
        out_specs=(VMEM,) * 3,
        scratch_shapes=[
            pltpu.VMEM(queries.shape, queries.dtype),
            pltpu.VMEM(keys.shape, keys.dtype),
            pltpu.VMEM(values.shape, values.dtype),
            pltpu.SemaphoreType.DMA((3,)),
        ],
        compiler_params=params,
        cost_estimate=cost(1),
        name="own",
    )(queries, keys, values)
    for distance in range(1, spans):
        waiting = [(distance - 1, t) for t in turned] + [(distance, tuple(held))]
        held, acc, stat = lax.optimization_barrier((held, acc, stat))
        waiting[-1] = (distance, tuple(held))
        turned, held = travel(held, distance)
        distances = [d for d, _ in waiting]

        count_in = 2 * len(waiting)
        blocks = [k for _, (k, _) in waiting] + [v for _, (_, v) in waiting]
        if distance == 1:

            def first_step(mask, section, gate, stacked, acc, stat, *refs, distances=distances):
                flag_kernel(per_span, mask, section, gate, *refs[-2:])
                step_kernel(distances, stacked, refs[-2], acc, stat, *refs[:-2])

            acc, stat, seen, gate_row = pl.pallas_call(
                first_step,
                out_shape=(
                    acc_shape, stat_shape, jax.ShapeDtypeStruct((spans, width), jnp.int32),
                    jax.ShapeDtypeStruct((1, wide), jnp.float32),
                ),
                in_specs=[pl.BlockSpec(memory_space=pltpu.SMEM)] * 2 + [VMEM] * (4 + count_in),
                out_specs=(VMEM,) * 4,
                compiler_params=params,
                cost_estimate=cost(len(waiting)),
                name="step_1",
            )(span_mask, section, section_gate, stacked, acc, stat, *blocks)
        else:

            def step(*refs, distances=distances):
                step_kernel(distances, *refs)

            acc, stat = pl.pallas_call(
                step,
                out_shape=(acc_shape, stat_shape),
                in_specs=[VMEM] * (4 + count_in),
                out_specs=(VMEM,) * 2,
                compiler_params=params,
                cost_estimate=cost(len(waiting)),
                name="step_%d" % distance,
            )(stacked, seen, acc, stat, *blocks)

    distances = [spans - 1] * len(turned)

    def close(*refs):
        close_kernel(distances, *refs)

    part, last_weight, log_total = pl.pallas_call(
        close,
        out_shape=(
            jax.ShapeDtypeStruct((kv_heads, width, HEAD_SIZE), jnp.float32),
            jax.ShapeDtypeStruct((kv_heads, width, len(turned) * rows), jnp.bfloat16),
            jax.ShapeDtypeStruct((heads, rows), jnp.float32),
        ),
        in_specs=[VMEM] * (5 + len(turned)),
        out_specs=(VMEM,) * 3,
        compiler_params=params,
        cost_estimate=cost(1),
        name="close",
    )(stacked, seen, gate_row, acc, stat, *[k for k, _ in turned])
    mixed = pl.pallas_call(
        mix_kernel,
        out_shape=jax.ShapeDtypeStruct((rows, wide), jnp.bfloat16),
        in_specs=[VMEM] * (3 + len(turned)),
        out_specs=HBM,
        scratch_shapes=[pltpu.VMEM((rows, wide), jnp.bfloat16), pltpu.SemaphoreType.DMA((kv_heads,))],
        compiler_params=params,
        cost_estimate=cost(1),
        name="mix",
    )(gate_row, part, last_weight, *[v for _, v in turned])
    return mixed, log_total


def solution(mesh):
    placed = (
        P(("grp", "tm"), "head"),
        P(("grp", "tm"), "head"),
        P(("grp", "tm"), "head"),
        P("grp", None),
        P("grp"),
        P(None, "head"),
    )
    return jax.shard_map(
        on_device,
        mesh=mesh,
        in_specs=placed,
        out_specs=(P(("grp", "tm"), "head"), P("head", ("grp", "tm"))),
        check_vma=False,
    )
```

```python
import math

import jax
import jax.numpy as jnp
from jax import lax
from jax.experimental import pallas as pl
from jax.experimental.pallas import tpu as pltpu
from jax.sharding import PartitionSpec as P

HEAD_SIZE = 128
CH = 256
LOG2E = math.log2(math.e)
LN2 = math.log(2.0)
FAR = 1e30
SCALE = LOG2E / math.sqrt(HEAD_SIZE)
HBM = pl.BlockSpec(memory_space=pltpu.HBM)
VMEM = pl.BlockSpec(memory_space=pltpu.VMEM)


def head_columns(h):
    return slice(h * HEAD_SIZE, (h + 1) * HEAD_SIZE)


def scores_of(k, queries):
    return SCALE * lax.dot_general(k, queries, (((1,), (1,)), ((), ())), preferred_element_type=jnp.float32)


def times_values(v, weight):
    return lax.dot_general(v, weight, (((0,), (0,)), ((), ())), preferred_element_type=jnp.float32)


def own_kernel(q_hbm, k_hbm, v_hbm, stacked, acc, stat, q, k, v, sems):
    copies = [
        pltpu.make_async_copy(src, dst, sems.at[i])
        for i, (src, dst) in enumerate([(q_hbm, q), (k_hbm, k), (v_hbm, v)])
    ]
    for copy in copies:
        copy.start()
    for copy in copies:
        copy.wait()
    rows = q.shape[0]
    group = stacked.shape[1] // rows
    for h in range(stacked.shape[0]):
        for g in range(group):
            stacked[h, g * rows : (g + 1) * rows, :] = q[:, head_columns(h * group + g)]
    for h in range(stacked.shape[0]):
        score = scores_of(k[:, head_columns(h)], stacked[h])
        top = jnp.max(score, axis=0, keepdims=True)
        weight = jnp.exp2(score - top)
        stat[h, 0:1, :] = top
        stat[h, 1:2, :] = jnp.sum(weight, axis=0, keepdims=True)
        acc[h] = times_values(v[:, head_columns(h)], weight.astype(jnp.bfloat16))


def flag_kernel(per_span, mask, section, gate, seen, gate_row):
    span = lax.axis_index("tm") // per_span
    for distance in range(seen.shape[0]):
        allowed = jnp.logical_and(span >= distance, mask[span, jnp.maximum(span - distance, 0)] > 0)
        seen[distance : distance + 1, :] = jnp.full((1, seen.shape[1]), allowed.astype(jnp.int32), jnp.int32)
    gate_row[...] = gate[pl.ds(section[span], 1), :]


def weigh(h, distances, stacked, seen, stat, key_refs):
    scores = [scores_of(k[:, head_columns(h)], stacked[h]) for k in key_refs]
    flags = [seen[d : d + 1, :] > 0 for d in distances]
    old = stat[h, 0:1, :]
    top = old
    for score, flag in zip(scores, flags):
        top = jnp.maximum(top, jnp.where(flag, jnp.max(score, axis=0, keepdims=True), -FAR))
    weights = [jnp.exp2(score - jnp.where(flag, top, FAR)) for score, flag in zip(scores, flags)]
    factor = jnp.exp2(old - top)
    total = stat[h, 1:2, :] * factor
    for weight in weights:
        total += jnp.sum(weight, axis=0, keepdims=True)
    return weights, top, total, factor


def step_kernel(distances, stacked, seen, acc_in, stat_in, *refs):
    count = len(distances)
    key_refs, value_refs, (acc, stat) = refs[:count], refs[count : 2 * count], refs[2 * count :]
    for h in range(stacked.shape[0]):
        weights, top, total, factor = weigh(h, distances, stacked, seen, stat_in, key_refs)
        stat[h, 0:1, :] = top
        stat[h, 1:2, :] = total
        acc[h] = acc_in[h] * factor + times_values(
            jnp.concatenate([v[:, head_columns(h)] for v in value_refs], axis=0),
            jnp.concatenate([weight.astype(jnp.bfloat16) for weight in weights], axis=0),
        )


def close_kernel(distances, stacked, seen, gate_row, acc_in, stat_in, *refs):
    key_refs, (part, last_weight, log_ref) = refs[: len(distances)], refs[len(distances) :]
    rows = log_ref.shape[1]
    group = stacked.shape[1] // rows
    for h in range(stacked.shape[0]):
        weights, top, total, factor = weigh(h, distances, stacked, seen, stat_in, key_refs)
        inverse = 1.0 / total
        log_total = top * LN2 + jnp.log(total)
        turned = (acc_in[h] * (factor * inverse)).T
        for at, weight in enumerate(weights):
            last_weight[h, :, head_columns(at)] = (weight * inverse).T.astype(jnp.bfloat16)
        for g in range(group):
            head = h * group + g
            inside = slice(g * rows, (g + 1) * rows)
            part[h, inside, :] = turned[inside, :] * gate_row[:, head_columns(head)]
            log_ref[head : head + 1, :] = log_total[:, inside]


def mix_kernel(gate_row, part, last_weight, *refs):
    value_refs, (mixed_hbm, mixed, sems) = refs[:-3], refs[-3:]
    kv_heads, width = part.shape[0], part.shape[1]
    rows = mixed.shape[0]
    group = width // rows
    copies = []
    for h in range(kv_heads):
        values = jnp.concatenate([v[:, head_columns(h)] for v in value_refs], axis=0)
        rest = jnp.dot(last_weight[h], values, preferred_element_type=jnp.float32)
        for g in range(group):
            inside = slice(g * rows, (g + 1) * rows)
            columns = head_columns(h * group + g)
            mixed[:, columns] = (part[h, inside, :] + gate_row[:, columns] * rest[inside, :]).astype(jnp.bfloat16)
        columns = pl.ds(h * group * HEAD_SIZE, group * HEAD_SIZE)
        copies.append(pltpu.make_async_copy(mixed.at[:, columns], mixed_hbm.at[:, columns], sems.at[h]))
        copies[-1].start()
    for copy in copies:
        copy.wait()


def on_device(queries, keys, values, span_mask, section, section_gate):
    rows, wide = queries.shape
    heads, kv_heads = wide // HEAD_SIZE, keys.shape[1] // HEAD_SIZE
    width = heads // kv_heads * rows
    count = lax.axis_size("tm")
    per_span = CH // rows
    spans = count // per_span
    params = pltpu.CompilerParams(vmem_limit_bytes=24 * 1024 * 1024)
    acc_shape = jax.ShapeDtypeStruct((kv_heads, HEAD_SIZE, width), jnp.float32)
    stat_shape = jax.ShapeDtypeStruct((kv_heads, 8, width), jnp.float32)

    def cost(blocks):
        return pl.CostEstimate(
            flops=40 * blocks * rows * rows * wide, bytes_accessed=rows * wide * 8, transcendentals=blocks * rows * rows * heads
        )

    def beside(i, turn):
        return i - i % per_span + (i + turn) % per_span

    def onward(value, distance):
        first = (distance - 1) * per_span
        pairs = [(i, beside(i, 1)) for i in range(first)] + [
            (i, i + per_span if i + per_span < count else first + i % per_span) for i in range(first, count)
        ]
        return lax.ppermute(value, "tm", pairs)

    def around(value, turn):
        return lax.ppermute(value, "tm", [(i, beside(i, turn)) for i in range(count)])

    def travel(held, distance):
        turned, onwards = [], []
        for x in held:
            if distance + 1 < spans:
                onwards.append(onward(x, distance + 1))
            turned.append([around(x, turn) for turn in range(1, per_span)])
        return list(zip(*turned)), onwards

    turned, held = travel((keys, values), 0)
    stacked, acc, stat = pl.pallas_call(
        own_kernel,
        out_shape=(jax.ShapeDtypeStruct((kv_heads, width, HEAD_SIZE), jnp.bfloat16), acc_shape, stat_shape),
        in_specs=[HBM] * 3,
        out_specs=(VMEM,) * 3,
        scratch_shapes=[
            pltpu.VMEM(queries.shape, queries.dtype),
            pltpu.VMEM(keys.shape, keys.dtype),
            pltpu.VMEM(values.shape, values.dtype),
            pltpu.SemaphoreType.DMA((3,)),
        ],
        compiler_params=params,
        cost_estimate=cost(1),
        name="own",
    )(queries, keys, values)
    for distance in range(1, spans):
        waiting = [(distance - 1, t) for t in turned] + [(distance, tuple(held))]
        held, acc, stat = lax.optimization_barrier((held, acc, stat))
        waiting[-1] = (distance, tuple(held))
        turned, held = travel(held, distance)
        distances = [d for d, _ in waiting]

        count_in = 2 * len(waiting)
        blocks = [k for _, (k, _) in waiting] + [v for _, (_, v) in waiting]
        if distance == 1:

            def first_step(mask, section, gate, stacked, acc, stat, *refs, distances=distances):
                flag_kernel(per_span, mask, section, gate, *refs[-2:])
                step_kernel(distances, stacked, refs[-2], acc, stat, *refs[:-2])

            acc, stat, seen, gate_row = pl.pallas_call(
                first_step,
                out_shape=(
                    acc_shape, stat_shape, jax.ShapeDtypeStruct((spans, width), jnp.int32),
                    jax.ShapeDtypeStruct((1, wide), jnp.float32),
                ),
                in_specs=[pl.BlockSpec(memory_space=pltpu.SMEM)] * 2 + [VMEM] * (4 + count_in),
                out_specs=(VMEM,) * 4,
                compiler_params=params,
                cost_estimate=cost(len(waiting)),
                name="step_1",
            )(span_mask, section, section_gate, stacked, acc, stat, *blocks)
        else:

            def step(*refs, distances=distances):
                step_kernel(distances, *refs)

            acc, stat = pl.pallas_call(
                step,
                out_shape=(acc_shape, stat_shape),
                in_specs=[VMEM] * (4 + count_in),
                out_specs=(VMEM,) * 2,
                compiler_params=params,
                cost_estimate=cost(len(waiting)),
                name="step_%d" % distance,
            )(stacked, seen, acc, stat, *blocks)

    distances = [spans - 1] * len(turned)

    def close(*refs):
        close_kernel(distances, *refs)

    part, last_weight, log_total = pl.pallas_call(
        close,
        out_shape=(
            jax.ShapeDtypeStruct((kv_heads, width, HEAD_SIZE), jnp.float32),
            jax.ShapeDtypeStruct((kv_heads, width, len(turned) * rows), jnp.bfloat16),
            jax.ShapeDtypeStruct((heads, rows), jnp.float32),
        ),
        in_specs=[VMEM] * (5 + len(turned)),
        out_specs=(VMEM,) * 3,
        compiler_params=params,
        cost_estimate=cost(1),
        name="close",
    )(stacked, seen, gate_row, acc, stat, *[k for k, _ in turned])
    mixed = pl.pallas_call(
        mix_kernel,
        out_shape=jax.ShapeDtypeStruct((rows, wide), jnp.bfloat16),
        in_specs=[VMEM] * (3 + len(turned)),
        out_specs=HBM,
        scratch_shapes=[pltpu.VMEM((rows, wide), jnp.bfloat16), pltpu.SemaphoreType.DMA((kv_heads,))],
        compiler_params=params,
        cost_estimate=cost(1),
        name="mix",
    )(gate_row, part, last_weight, *[v for _, v in turned])
    return mixed, log_total


def solution(mesh):
    placed = (
        P(("grp", "tm"), "head"),
        P(("grp", "tm"), "head"),
        P(("grp", "tm"), "head"),
        P("grp", None),
        P("grp"),
        P(None, "head"),
    )
    return jax.shard_map(
        on_device,
        mesh=mesh,
        in_specs=placed,
        out_specs=(P(("grp", "tm"), "head"), P("head", ("grp", "tm"))),
        check_vma=False,
    )
```

```python
import math

import jax
import jax.numpy as jnp
from jax import lax
from jax.experimental import pallas as pl
from jax.experimental.pallas import tpu as pltpu
from jax.sharding import PartitionSpec as P

HEAD_SIZE = 128
CH = 256
LOG2E = math.log2(math.e)
LN2 = math.log(2.0)
FAR = 1e30
SCALE = LOG2E / math.sqrt(HEAD_SIZE)
HBM = pl.BlockSpec(memory_space=pltpu.HBM)
VMEM = pl.BlockSpec(memory_space=pltpu.VMEM)


def head_columns(h):
    return slice(h * HEAD_SIZE, (h + 1) * HEAD_SIZE)


def scores_of(k, queries):
    return SCALE * lax.dot_general(k, queries, (((1,), (1,)), ((), ())), preferred_element_type=jnp.float32)


def times_values(v, weight):
    return lax.dot_general(v, weight, (((0,), (0,)), ((), ())), preferred_element_type=jnp.float32)


def floor_kernel(floor):
    floor[...] = jnp.full(floor.shape, -FAR, jnp.float32)


def own_kernel(floor, q_hbm, k_hbm, v_hbm, stacked, acc, stat, q, k, v, sems):
    copies = [
        pltpu.make_async_copy(src, dst, sems.at[i])
        for i, (src, dst) in enumerate([(q_hbm, q), (k_hbm, k), (v_hbm, v)])
    ]
    for copy in copies:
        copy.start()
    for copy in copies:
        copy.wait()
    rows = q.shape[0]
    group = stacked.shape[1] // rows
    for h in range(stacked.shape[0]):
        for g in range(group):
            stacked[h, g * rows : (g + 1) * rows, :] = q[:, head_columns(h * group + g)]
    for h in range(stacked.shape[0]):
        score = scores_of(k[:, head_columns(h)], stacked[h])
        top = jnp.maximum(floor[0:1, :], jnp.max(score, axis=0, keepdims=True))
        weight = jnp.exp2(score - top)
        stat[h, 0:1, :] = top
        stat[h, 1:2, :] = jnp.sum(weight, axis=0, keepdims=True)
        acc[h] = times_values(v[:, head_columns(h)], weight.astype(jnp.bfloat16))


def flag_kernel(per_span, mask, section, gate, seen, gate_row):
    span = lax.axis_index("tm") // per_span
    for distance in range(seen.shape[0]):
        allowed = jnp.logical_and(span >= distance, mask[span, jnp.maximum(span - distance, 0)] > 0)
        seen[distance : distance + 1, :] = jnp.full((1, seen.shape[1]), allowed.astype(jnp.int32), jnp.int32)
    gate_row[...] = gate[pl.ds(section[span], 1), :]


def weigh(h, distances, stacked, seen, stat, key_refs):
    scores = [scores_of(k[:, head_columns(h)], stacked[h]) for k in key_refs]
    flags = [seen[d : d + 1, :] > 0 for d in distances]
    old = stat[h, 0:1, :]
    top = old
    for score, flag in zip(scores, flags):
        top = jnp.maximum(top, jnp.where(flag, jnp.max(score, axis=0, keepdims=True), -FAR))
    weights = [jnp.exp2(score - jnp.where(flag, top, FAR)) for score, flag in zip(scores, flags)]
    factor = jnp.exp2(old - top)
    total = stat[h, 1:2, :] * factor
    for weight in weights:
        total += jnp.sum(weight, axis=0, keepdims=True)
    return weights, top, total, factor


def step_kernel(distances, stacked, seen, acc_in, stat_in, *refs):
    count = len(distances)
    key_refs, value_refs, (acc, stat) = refs[:count], refs[count : 2 * count], refs[2 * count :]
    for h in range(stacked.shape[0]):
        weights, top, total, factor = weigh(h, distances, stacked, seen, stat_in, key_refs)
        stat[h, 0:1, :] = top
        stat[h, 1:2, :] = total
        acc[h] = acc_in[h] * factor + times_values(
            jnp.concatenate([v[:, head_columns(h)] for v in value_refs], axis=0),
            jnp.concatenate([weight.astype(jnp.bfloat16) for weight in weights], axis=0),
        )


def close_kernel(distances, stacked, seen, gate_row, acc_in, stat_in, *refs):
    key_refs, (part, last_weight, log_ref) = refs[: len(distances)], refs[len(distances) :]
    rows = log_ref.shape[1]
    group = stacked.shape[1] // rows
    for h in range(stacked.shape[0]):
        weights, top, total, factor = weigh(h, distances, stacked, seen, stat_in, key_refs)
        inverse = 1.0 / total
        log_total = top * LN2 + jnp.log(total)
        turned = (acc_in[h] * (factor * inverse)).T
        for at, weight in enumerate(weights):
            last_weight[h, :, head_columns(at)] = (weight * inverse).T.astype(jnp.bfloat16)
        for g in range(group):
            head = h * group + g
            inside = slice(g * rows, (g + 1) * rows)
            part[h, inside, :] = turned[inside, :] * gate_row[:, head_columns(head)]
            log_ref[head : head + 1, :] = log_total[:, inside]


def mix_kernel(gate_row, part, last_weight, *refs):
    value_refs, (mixed_hbm, mixed, sems) = refs[:-3], refs[-3:]
    kv_heads, width = part.shape[0], part.shape[1]
    rows = mixed.shape[0]
    group = width // rows
    copies = []
    for h in range(kv_heads):
        values = jnp.concatenate([v[:, head_columns(h)] for v in value_refs], axis=0)
        rest = jnp.dot(last_weight[h], values, preferred_element_type=jnp.float32)
        for g in range(group):
            inside = slice(g * rows, (g + 1) * rows)
            columns = head_columns(h * group + g)
            mixed[:, columns] = (part[h, inside, :] + gate_row[:, columns] * rest[inside, :]).astype(jnp.bfloat16)
        columns = pl.ds(h * group * HEAD_SIZE, group * HEAD_SIZE)
        copies.append(pltpu.make_async_copy(mixed.at[:, columns], mixed_hbm.at[:, columns], sems.at[h]))
        copies[-1].start()
    for copy in copies:
        copy.wait()


def on_device(queries, keys, values, span_mask, section, section_gate):
    rows, wide = queries.shape
    heads, kv_heads = wide // HEAD_SIZE, keys.shape[1] // HEAD_SIZE
    width = heads // kv_heads * rows
    count = lax.axis_size("tm")
    per_span = CH // rows
    spans = count // per_span
    params = pltpu.CompilerParams(vmem_limit_bytes=24 * 1024 * 1024)
    acc_shape = jax.ShapeDtypeStruct((kv_heads, HEAD_SIZE, width), jnp.float32)
    stat_shape = jax.ShapeDtypeStruct((kv_heads, 8, width), jnp.float32)

    def cost(blocks):
        return pl.CostEstimate(
            flops=40 * blocks * rows * rows * wide, bytes_accessed=rows * wide * 8, transcendentals=blocks * rows * rows * heads
        )

    cores = lax.axis_size("head")

    def send(value, target):
        pairs = []
        for i in range(count):
            for core in range(cores):
                if target(i) is None:
                    goal = i * cores + (core + 1) % cores if cores > 1 else i
                else:
                    goal = target(i) * cores + core
                pairs.append((i * cores + core, goal))
        return lax.ppermute(value, ("tm", "head"), pairs)

    def onward(value, distance):
        first = (distance - 1) * per_span

        def target(i):
            if i < first:
                return None
            return i + per_span if i + per_span < count else first + i % per_span

        return send(value, target)

    def around(value, distance, turn):
        return send(
            value, lambda i: i - i % per_span + (i + turn) % per_span if i >= distance * per_span else None
        )

    def travel(held, distance):
        turned, onwards = [], []
        for x in held:
            if distance + 1 < spans:
                onwards.append(onward(x, distance + 1))
            turned.append([around(x, distance, turn) for turn in range(1, per_span)])
        return list(zip(*turned)), onwards

    turned, held = travel((keys, values), 0)
    floor = pl.pallas_call(
        floor_kernel,
        out_shape=jax.ShapeDtypeStruct((8, width), jnp.float32),
        out_specs=VMEM,
        compiler_params=params,
        cost_estimate=cost(4),
        name="floor",
    )()
    stacked, acc, stat = pl.pallas_call(
        own_kernel,
        out_shape=(jax.ShapeDtypeStruct((kv_heads, width, HEAD_SIZE), jnp.bfloat16), acc_shape, stat_shape),
        in_specs=[VMEM] + [HBM] * 3,
        out_specs=(VMEM,) * 3,
        scratch_shapes=[
            pltpu.VMEM(queries.shape, queries.dtype),
            pltpu.VMEM(keys.shape, keys.dtype),
            pltpu.VMEM(values.shape, values.dtype),
            pltpu.SemaphoreType.DMA((3,)),
        ],
        compiler_params=params,
        cost_estimate=cost(1),
        name="own",
    )(floor, queries, keys, values)
    for distance in range(1, spans):
        waiting = [(distance - 1, t) for t in turned] + [(distance, tuple(held))]
        forward = []
        for x in held:
            x, stat = lax.optimization_barrier((x, stat))
            forward.append(x)
        held = forward
        waiting[-1] = (distance, tuple(held))
        turned, held = travel(held, distance)
        distances = [d for d, _ in waiting]

        count_in = 2 * len(waiting)
        blocks = [k for _, (k, _) in waiting] + [v for _, (_, v) in waiting]
        if distance == 1:

            def first_step(mask, section, gate, stacked, acc, stat, *refs, distances=distances):
                flag_kernel(per_span, mask, section, gate, *refs[-2:])
                step_kernel(distances, stacked, refs[-2], acc, stat, *refs[:-2])

            acc, stat, seen, gate_row = pl.pallas_call(
                first_step,
                out_shape=(
                    acc_shape, stat_shape, jax.ShapeDtypeStruct((spans, width), jnp.int32),
                    jax.ShapeDtypeStruct((1, wide), jnp.float32),
                ),
                in_specs=[pl.BlockSpec(memory_space=pltpu.SMEM)] * 2 + [VMEM] * (4 + count_in),
                out_specs=(VMEM,) * 4,
                compiler_params=params,
                cost_estimate=cost(len(waiting)),
                name="step_1",
            )(span_mask, section, section_gate, stacked, acc, stat, *blocks)
        else:

            def step(*refs, distances=distances):
                step_kernel(distances, *refs)

            acc, stat = pl.pallas_call(
                step,
                out_shape=(acc_shape, stat_shape),
                in_specs=[VMEM] * (4 + count_in),
                out_specs=(VMEM,) * 2,
                compiler_params=params,
                cost_estimate=cost(len(waiting)),
                name="step_%d" % distance,
            )(stacked, seen, acc, stat, *blocks)

    distances = [spans - 1] * len(turned)

    def close(*refs):
        close_kernel(distances, *refs)

    part, last_weight, log_total = pl.pallas_call(
        close,
        out_shape=(
            jax.ShapeDtypeStruct((kv_heads, width, HEAD_SIZE), jnp.float32),
            jax.ShapeDtypeStruct((kv_heads, width, len(turned) * rows), jnp.bfloat16),
            jax.ShapeDtypeStruct((heads, rows), jnp.float32),
        ),
        in_specs=[VMEM] * (5 + len(turned)),
        out_specs=(VMEM,) * 3,
        compiler_params=params,
        cost_estimate=cost(1),
        name="close",
    )(stacked, seen, gate_row, acc, stat, *[k for k, _ in turned])
    mixed = pl.pallas_call(
        mix_kernel,
        out_shape=jax.ShapeDtypeStruct((rows, wide), jnp.bfloat16),
        in_specs=[VMEM] * (3 + len(turned)),
        out_specs=HBM,
        scratch_shapes=[pltpu.VMEM((rows, wide), jnp.bfloat16), pltpu.SemaphoreType.DMA((kv_heads,))],
        compiler_params=params,
        cost_estimate=cost(1),
        name="mix",
    )(gate_row, part, last_weight, *[v for _, v in turned])
    return mixed, log_total


def solution(mesh):
    placed = (
        P(("grp", "tm"), "head"),
        P(("grp", "tm"), "head"),
        P(("grp", "tm"), "head"),
        P("grp", None),
        P("grp"),
        P(None, "head"),
    )
    return jax.shard_map(
        on_device,
        mesh=mesh,
        in_specs=placed,
        out_specs=(P(("grp", "tm"), "head"), P("head", ("grp", "tm"))),
        check_vma=False,
    )
```

```python
import math

import jax
import jax.numpy as jnp
from jax import lax
from jax.experimental import pallas as pl
from jax.experimental.pallas import tpu as pltpu
from jax.sharding import PartitionSpec as P

HEAD_SIZE = 128
CH = 256
LOG2E = math.log2(math.e)
LN2 = math.log(2.0)
FAR = 1e30
SCALE = LOG2E / math.sqrt(HEAD_SIZE)
HBM = pl.BlockSpec(memory_space=pltpu.HBM)
VMEM = pl.BlockSpec(memory_space=pltpu.VMEM)


def head_columns(h):
    return slice(h * HEAD_SIZE, (h + 1) * HEAD_SIZE)


def scores_of(k, queries):
    return SCALE * lax.dot_general(k, queries, (((1,), (1,)), ((), ())), preferred_element_type=jnp.float32)


def times_values(v, weight):
    return lax.dot_general(v, weight, (((0,), (0,)), ((), ())), preferred_element_type=jnp.float32)


def floor_kernel(floor):
    floor[...] = jnp.full(floor.shape, -FAR, jnp.float32)


def own_kernel(floor, q_hbm, k_hbm, v_hbm, stacked, acc, stat, q, k, v, sems):
    copies = [
        pltpu.make_async_copy(src, dst, sems.at[i])
        for i, (src, dst) in enumerate([(q_hbm, q), (k_hbm, k), (v_hbm, v)])
    ]
    for copy in copies:
        copy.start()
    for copy in copies:
        copy.wait()
    rows = q.shape[0]
    group = stacked.shape[1] // rows
    for h in range(stacked.shape[0]):
        for g in range(group):
            stacked[h, g * rows : (g + 1) * rows, :] = q[:, head_columns(h * group + g)]
    for h in range(stacked.shape[0]):
        score = scores_of(k[:, head_columns(h)], stacked[h])
        top = jnp.maximum(floor[0:1, :], jnp.max(score, axis=0, keepdims=True))
        weight = jnp.exp2(score - top)
        stat[h, 0:1, :] = top
        stat[h, 1:2, :] = jnp.sum(weight, axis=0, keepdims=True)
        acc[h] = times_values(v[:, head_columns(h)], weight.astype(jnp.bfloat16))


def flag_kernel(per_span, mask, section, gate, seen, gate_row):
    span = lax.axis_index("tm") // per_span
    for distance in range(seen.shape[0]):
        allowed = jnp.logical_and(span >= distance, mask[span, jnp.maximum(span - distance, 0)] > 0)
        seen[distance : distance + 1, :] = jnp.full((1, seen.shape[1]), allowed.astype(jnp.int32), jnp.int32)
    gate_row[...] = gate[pl.ds(section[span], 1), :]


def weigh(h, distances, stacked, seen, stat, key_refs):
    scores = [scores_of(k[:, head_columns(h)], stacked[h]) for k in key_refs]
    flags = [seen[d : d + 1, :] > 0 for d in distances]
    old = stat[h, 0:1, :]
    top = old
    for score, flag in zip(scores, flags):
        top = jnp.maximum(top, jnp.where(flag, jnp.max(score, axis=0, keepdims=True), -FAR))
    weights = [jnp.exp2(score - jnp.where(flag, top, FAR)) for score, flag in zip(scores, flags)]
    factor = jnp.exp2(old - top)
    total = stat[h, 1:2, :] * factor
    for weight in weights:
        total += jnp.sum(weight, axis=0, keepdims=True)
    return weights, top, total, factor


def step_kernel(distances, stacked, seen, acc_in, stat_in, *refs):
    count = len(distances)
    key_refs, value_refs, (acc, stat) = refs[:count], refs[count : 2 * count], refs[2 * count :]
    for h in range(stacked.shape[0]):
        weights, top, total, factor = weigh(h, distances, stacked, seen, stat_in, key_refs)
        stat[h, 0:1, :] = top
        stat[h, 1:2, :] = total
        acc[h] = acc_in[h] * factor + times_values(
            jnp.concatenate([v[:, head_columns(h)] for v in value_refs], axis=0),
            jnp.concatenate([weight.astype(jnp.bfloat16) for weight in weights], axis=0),
        )


def close_kernel(distances, stacked, seen, gate_row, acc_in, stat_in, *refs):
    key_refs, (part, last_weight, log_ref) = refs[: len(distances)], refs[len(distances) :]
    rows = log_ref.shape[1]
    group = stacked.shape[1] // rows
    for h in range(stacked.shape[0]):
        weights, top, total, factor = weigh(h, distances, stacked, seen, stat_in, key_refs)
        inverse = 1.0 / total
        log_total = top * LN2 + jnp.log(total)
        turned = (acc_in[h] * (factor * inverse)).T
        for at, weight in enumerate(weights):
            last_weight[h, :, head_columns(at)] = (weight * inverse).T.astype(jnp.bfloat16)
        for g in range(group):
            head = h * group + g
            inside = slice(g * rows, (g + 1) * rows)
            part[h, inside, :] = turned[inside, :] * gate_row[:, head_columns(head)]
            log_ref[head : head + 1, :] = log_total[:, inside]


def mix_kernel(gate_row, part, last_weight, *refs):
    value_refs, (mixed_hbm, mixed, sems) = refs[:-3], refs[-3:]
    kv_heads, width = part.shape[0], part.shape[1]
    rows = mixed.shape[0]
    group = width // rows
    copies = []
    for h in range(kv_heads):
        values = jnp.concatenate([v[:, head_columns(h)] for v in value_refs], axis=0)
        rest = jnp.dot(last_weight[h], values, preferred_element_type=jnp.float32)
        for g in range(group):
            inside = slice(g * rows, (g + 1) * rows)
            columns = head_columns(h * group + g)
            mixed[:, columns] = (part[h, inside, :] + gate_row[:, columns] * rest[inside, :]).astype(jnp.bfloat16)
        columns = pl.ds(h * group * HEAD_SIZE, group * HEAD_SIZE)
        copies.append(pltpu.make_async_copy(mixed.at[:, columns], mixed_hbm.at[:, columns], sems.at[h]))
        copies[-1].start()
    for copy in copies:
        copy.wait()


def on_device(queries, keys, values, span_mask, section, section_gate):
    rows, wide = queries.shape
    heads, kv_heads = wide // HEAD_SIZE, keys.shape[1] // HEAD_SIZE
    width = heads // kv_heads * rows
    count = lax.axis_size("tm")
    per_span = CH // rows
    spans = count // per_span
    params = pltpu.CompilerParams(vmem_limit_bytes=24 * 1024 * 1024)
    acc_shape = jax.ShapeDtypeStruct((kv_heads, HEAD_SIZE, width), jnp.float32)
    stat_shape = jax.ShapeDtypeStruct((kv_heads, 8, width), jnp.float32)

    def cost(blocks, times=2):
        return pl.CostEstimate(
            flops=4 * times * blocks * rows * rows * wide, bytes_accessed=rows * wide * 8, transcendentals=blocks * rows * rows * heads
        )

    cores = lax.axis_size("head")

    def send(value, target):
        pairs = []
        for i in range(count):
            for core in range(cores):
                if target(i) is None:
                    goal = i * cores + (core + 1) % cores if cores > 1 else i
                else:
                    goal = target(i) * cores + core
                pairs.append((i * cores + core, goal))
        return lax.ppermute(value, ("tm", "head"), pairs)

    def onward(value, distance):
        first = (distance - 1) * per_span

        def target(i):
            if i < first:
                return None
            return i + per_span if i + per_span < count else first + i % per_span

        return send(value, target)

    def around(value, distance, turn):
        return send(
            value, lambda i: i - i % per_span + (i + turn) % per_span if i >= distance * per_span else None
        )

    def travel(held, distance, turned_before):
        onwards = [onward(x, distance + 1) for x in held] if distance + 1 < spans else []
        turned = [[around(x, distance, turn) for turn in range(1, per_span)] for x in held]
        if not onwards and turned_before:
            turned[1] = [onward(v, distance) for _, v in turned_before]
        return list(zip(*turned)), onwards

    floor = pl.pallas_call(
        floor_kernel,
        out_shape=jax.ShapeDtypeStruct((8, width), jnp.float32),
        out_specs=VMEM,
        compiler_params=params,
        cost_estimate=cost(4, 10),
        name="floor",
    )()
    held = [onward(x, 1) for x in (keys, values)] if spans > 1 else []
    near_keys, near_values, floor = lax.optimization_barrier((keys, values, floor))
    turned = list(zip(*[[around(x, 0, turn) for turn in range(1, per_span)] for x in (near_keys, near_values)]))
    stacked, acc, stat = pl.pallas_call(
        own_kernel,
        out_shape=(jax.ShapeDtypeStruct((kv_heads, width, HEAD_SIZE), jnp.bfloat16), acc_shape, stat_shape),
        in_specs=[VMEM] + [HBM] * 3,
        out_specs=(VMEM,) * 3,
        scratch_shapes=[
            pltpu.VMEM(queries.shape, queries.dtype),
            pltpu.VMEM(keys.shape, keys.dtype),
            pltpu.VMEM(values.shape, values.dtype),
            pltpu.SemaphoreType.DMA((3,)),
        ],
        compiler_params=params,
        cost_estimate=cost(1, 10),
        name="own",
    )(floor, queries, keys, values)
    for distance in range(1, spans):
        waiting = [(distance - 1, t) for t in turned] + [(distance, tuple(held))]
        forward = []
        for x in held:
            x, stat = lax.optimization_barrier((x, stat))
            forward.append(x)
        held = forward
        waiting[-1] = (distance, tuple(held))
        turned, held = travel(held, distance, turned)
        distances = [d for d, _ in waiting]

        count_in = 2 * len(waiting)
        blocks = [k for _, (k, _) in waiting] + [v for _, (_, v) in waiting]
        if distance == 1:

            def first_step(mask, section, gate, stacked, acc, stat, *refs, distances=distances):
                flag_kernel(per_span, mask, section, gate, *refs[-2:])
                step_kernel(distances, stacked, refs[-2], acc, stat, *refs[:-2])

            acc, stat, seen, gate_row = pl.pallas_call(
                first_step,
                out_shape=(
                    acc_shape, stat_shape, jax.ShapeDtypeStruct((spans, width), jnp.int32),
                    jax.ShapeDtypeStruct((1, wide), jnp.float32),
                ),
                in_specs=[pl.BlockSpec(memory_space=pltpu.SMEM)] * 2 + [VMEM] * (4 + count_in),
                out_specs=(VMEM,) * 4,
                compiler_params=params,
                cost_estimate=cost(len(waiting)),
                name="step_1",
            )(span_mask, section, section_gate, stacked, acc, stat, *blocks)
        else:

            def step(*refs, distances=distances):
                step_kernel(distances, *refs)

            acc, stat = pl.pallas_call(
                step,
                out_shape=(acc_shape, stat_shape),
                in_specs=[VMEM] * (4 + count_in),
                out_specs=(VMEM,) * 2,
                compiler_params=params,
                cost_estimate=cost(len(waiting)),
                name="step_%d" % distance,
            )(stacked, seen, acc, stat, *blocks)

    distances = [spans - 1] * len(turned)

    def close(*refs):
        close_kernel(distances, *refs)

    part, last_weight, log_total = pl.pallas_call(
        close,
        out_shape=(
            jax.ShapeDtypeStruct((kv_heads, width, HEAD_SIZE), jnp.float32),
            jax.ShapeDtypeStruct((kv_heads, width, len(turned) * rows), jnp.bfloat16),
            jax.ShapeDtypeStruct((heads, rows), jnp.float32),
        ),
        in_specs=[VMEM] * (5 + len(turned)),
        out_specs=(VMEM,) * 3,
        compiler_params=params,
        cost_estimate=cost(1),
        name="close",
    )(stacked, seen, gate_row, acc, stat, *[k for k, _ in turned])
    mixed = pl.pallas_call(
        mix_kernel,
        out_shape=jax.ShapeDtypeStruct((rows, wide), jnp.bfloat16),
        in_specs=[VMEM] * (3 + len(turned)),
        out_specs=HBM,
        scratch_shapes=[pltpu.VMEM((rows, wide), jnp.bfloat16), pltpu.SemaphoreType.DMA((kv_heads,))],
        compiler_params=params,
        cost_estimate=cost(1),
        name="mix",
    )(gate_row, part, last_weight, *[v for _, v in turned])
    return mixed, log_total


def solution(mesh):
    placed = (
        P(("grp", "tm"), "head"),
        P(("grp", "tm"), "head"),
        P(("grp", "tm"), "head"),
        P("grp", None),
        P("grp"),
        P(None, "head"),
    )
    return jax.shard_map(
        on_device,
        mesh=mesh,
        in_specs=placed,
        out_specs=(P(("grp", "tm"), "head"), P("head", ("grp", "tm"))),
        check_vma=False,
    )
```

```python
import math

import jax
import jax.numpy as jnp
from jax import lax
from jax.experimental import pallas as pl
from jax.experimental.pallas import tpu as pltpu
from jax.sharding import PartitionSpec as P

HEAD_SIZE = 128
CH = 256
LOG2E = math.log2(math.e)
LN2 = math.log(2.0)
FAR = 1e30
LIMIT = 2.0**80
SCALE = LOG2E / math.sqrt(HEAD_SIZE)
HBM = pl.BlockSpec(memory_space=pltpu.HBM)
VMEM = pl.BlockSpec(memory_space=pltpu.VMEM)


def head_columns(h):
    return slice(h * HEAD_SIZE, (h + 1) * HEAD_SIZE)


def scores_of(k, queries):
    return lax.dot_general(k, queries, (((1,), (1,)), ((), ())), preferred_element_type=jnp.float32)


def times_values(v, weight):
    return lax.dot_general(v, weight, (((0,), (0,)), ((), ())), preferred_element_type=jnp.float32)


def floor_kernel(floor):
    floor[...] = jnp.full(floor.shape, -FAR, jnp.float32)


def own_kernel(per_span, mask, section, gate, floor, q_hbm, k_hbm, v_hbm,
               stacked, seen, gate_row, acc, stat, q, k, v, sems):
    copies = [
        pltpu.make_async_copy(src, dst, sems.at[i])
        for i, (src, dst) in enumerate([(q_hbm, q), (k_hbm, k), (v_hbm, v)])
    ]
    for copy in copies:
        copy.start()
    span = lax.axis_index("tm") // per_span
    for distance in range(seen.shape[0]):
        allowed = jnp.logical_and(span >= distance, mask[span, jnp.maximum(span - distance, 0)] > 0)
        seen[distance : distance + 1, :] = jnp.full((1, seen.shape[1]), allowed.astype(jnp.int32), jnp.int32)
    gate_row[...] = gate[pl.ds(section[span], 1), :]
    for copy in copies:
        copy.wait()
    rows = q.shape[0]
    group = stacked.shape[1] // rows
    for h in range(stacked.shape[0]):
        for g in range(group):
            stacked[h, g * rows : (g + 1) * rows, :] = q[:, head_columns(h * group + g)]
    for h in range(stacked.shape[0]):
        score = SCALE * scores_of(k[:, head_columns(h)], stacked[h])
        top = jnp.maximum(floor[0:1, :], jnp.max(score, axis=0, keepdims=True))
        weight = jnp.exp2(score - top)
        stat[h, 0:1, :] = top
        stat[h, 1:2, :] = jnp.sum(weight, axis=0, keepdims=True)
        acc[h] = times_values(v[:, head_columns(h)], weight.astype(jnp.bfloat16))


def chunks_of(width):
    size = 256 if width % 256 == 0 else width
    return [slice(at, at + size) for at in range(0, width, size)]


def weigh(exact, h, inside, distances, stacked, seen, stat, key_refs):
    scores = [scores_of(k[:, head_columns(h)], stacked[h, inside, :]) for k in key_refs]
    flags = [seen[d : d + 1, inside] > 0 for d in distances]
    old = stat[h, 0:1, inside]
    top = old
    if exact:
        for score, flag in zip(scores, flags):
            top = jnp.maximum(top, jnp.where(flag, SCALE * jnp.max(score, axis=0, keepdims=True), -FAR))
    weights = [jnp.exp2(SCALE * score - jnp.where(flag, top, FAR)) for score, flag in zip(scores, flags)]
    factor = jnp.exp2(old - top) if exact else None
    total = stat[h, 1:2, inside]
    if exact:
        total *= factor
    for weight in weights:
        total += jnp.sum(weight, axis=0, keepdims=True)
    return weights, top, total, factor


def with_check(work):
    largest = None
    within = None
    for total in work(False):
        fits = jnp.where(total <= LIMIT, 0.0, 1.0)
        within = fits if within is None else within + fits
    largest = jnp.max(within)

    @pl.when(largest > 0.0)
    def _():
        work(True)


def step_kernel(distances, stacked, seen, acc_in, stat_in, *refs):
    count = len(distances)
    key_refs, value_refs, (acc, stat) = refs[:count], refs[count : 2 * count], refs[2 * count :]

    def work(exact):
        totals = []
        for h in range(stacked.shape[0]):
            values = jnp.concatenate([v[:, head_columns(h)] for v in value_refs], axis=0)
            for inside in chunks_of(stacked.shape[1]):
                weights, top, total, factor = weigh(exact, h, inside, distances, stacked, seen, stat_in, key_refs)
                stat[h, 0:1, inside] = top
                stat[h, 1:2, inside] = total
                state = acc_in[h, :, inside] * factor if exact else acc_in[h, :, inside]
                acc[h, :, inside] = state + times_values(
                    values, jnp.concatenate([weight.astype(jnp.bfloat16) for weight in weights], axis=0)
                )
                totals.append(total)
        return totals

    with_check(work)


def close_kernel(distances, stacked, seen, gate_row, acc_in, stat_in, *refs):
    key_refs, (part, last_weight, log_ref) = refs[: len(distances)], refs[len(distances) :]
    rows = log_ref.shape[1]

    def work(exact):
        totals = []
        for h in range(stacked.shape[0]):
            for inside in chunks_of(stacked.shape[1]):
                weights, top, total, factor = weigh(exact, h, inside, distances, stacked, seen, stat_in, key_refs)
                inverse = 1.0 / total
                log_total = top * LN2 + jnp.log(total)
                turned = (acc_in[h, :, inside] * (factor * inverse if exact else inverse)).T
                for at, weight in enumerate(weights):
                    last_weight[h, inside, head_columns(at)] = (weight * inverse).T.astype(jnp.bfloat16)
                for at in range(0, turned.shape[0], rows):
                    head = (h * stacked.shape[1] + inside.start + at) // rows
                    part[h, inside.start + at : inside.start + at + rows, :] = (
                        turned[at : at + rows, :] * gate_row[:, head_columns(head)]
                    )
                    log_ref[head : head + 1, :] = log_total[:, at : at + rows]
                totals.append(total)
        return totals

    with_check(work)


def mix_kernel(gate_row, part, last_weight, *refs):
    value_refs, (mixed_hbm, mixed, sems) = refs[:-3], refs[-3:]
    kv_heads, width = part.shape[0], part.shape[1]
    rows = mixed.shape[0]
    group = width // rows
    copies = []
    for h in range(kv_heads):
        values = jnp.concatenate([v[:, head_columns(h)] for v in value_refs], axis=0)
        rest = jnp.dot(last_weight[h], values, preferred_element_type=jnp.float32)
        for g in range(group):
            inside = slice(g * rows, (g + 1) * rows)
            columns = head_columns(h * group + g)
            mixed[:, columns] = (part[h, inside, :] + gate_row[:, columns] * rest[inside, :]).astype(jnp.bfloat16)
        columns = pl.ds(h * group * HEAD_SIZE, group * HEAD_SIZE)
        copies.append(pltpu.make_async_copy(mixed.at[:, columns], mixed_hbm.at[:, columns], sems.at[h]))
        copies[-1].start()
    for copy in copies:
        copy.wait()


def on_device(queries, keys, values, span_mask, section, section_gate):
    rows, wide = queries.shape
    heads, kv_heads = wide // HEAD_SIZE, keys.shape[1] // HEAD_SIZE
    width = heads // kv_heads * rows
    count = lax.axis_size("tm")
    per_span = CH // rows
    spans = count // per_span
    params = pltpu.CompilerParams(vmem_limit_bytes=24 * 1024 * 1024)
    acc_shape = jax.ShapeDtypeStruct((kv_heads, HEAD_SIZE, width), jnp.float32)
    stat_shape = jax.ShapeDtypeStruct((kv_heads, 8, width), jnp.float32)

    def cost(blocks, times=2):
        return pl.CostEstimate(
            flops=4 * times * blocks * rows * rows * wide, bytes_accessed=rows * wide * 8, transcendentals=blocks * rows * rows * heads
        )

    cores = lax.axis_size("head")

    def send(value, target):
        pairs = []
        for i in range(count):
            for core in range(cores):
                if target(i) is None:
                    goal = i * cores + (core + 1) % cores if cores > 1 else i
                else:
                    goal = target(i) * cores + core
                pairs.append((i * cores + core, goal))
        return lax.ppermute(value, ("tm", "head"), pairs)

    def onward(value, distance):
        first = (max(min(distance - 1, spans - 3), 0) if distance > 1 else 0) * per_span

        def target(i):
            if i < first:
                return None
            return i + per_span if i + per_span < count else first + i % per_span

        return send(value, target)

    def around(value, distance, turn):
        return send(
            value, lambda i: i - i % per_span + (i + turn) % per_span if i >= distance * per_span else None
        )

    def travel(held, distance, turned_before):
        onwards = [onward(x, distance + 1) for x in held] if distance + 1 < spans else []
        turned = [[around(x, distance, turn) for turn in range(1, per_span)] for x in held]
        if not onwards and turned_before:
            turned[1] = [onward(v, distance) for _, v in turned_before]
        return list(zip(*turned)), onwards

    floor = pl.pallas_call(
        floor_kernel,
        out_shape=jax.ShapeDtypeStruct((8, width), jnp.float32),
        out_specs=VMEM,
        compiler_params=params,
        cost_estimate=cost(4, 10),
        name="floor",
    )()
    held = [onward(x, 1) for x in (keys, values)] if spans > 1 else []
    near_keys, near_values, floor = lax.optimization_barrier((keys, values, floor))
    turned = list(zip(*[[around(x, 0, turn) for turn in range(1, per_span)] for x in (near_keys, near_values)]))
    def own(*refs):
        own_kernel(per_span, *refs)

    stacked, seen, gate_row, acc, stat = pl.pallas_call(
        own,
        out_shape=(
            jax.ShapeDtypeStruct((kv_heads, width, HEAD_SIZE), jnp.bfloat16),
            jax.ShapeDtypeStruct((spans, width), jnp.int32),
            jax.ShapeDtypeStruct((1, wide), jnp.float32),
            acc_shape,
            stat_shape,
        ),
        in_specs=[pl.BlockSpec(memory_space=pltpu.SMEM)] * 2 + [VMEM] * 2 + [HBM] * 3,
        out_specs=(VMEM,) * 5,
        scratch_shapes=[
            pltpu.VMEM(queries.shape, queries.dtype),
            pltpu.VMEM(keys.shape, keys.dtype),
            pltpu.VMEM(values.shape, values.dtype),
            pltpu.SemaphoreType.DMA((3,)),
        ],
        compiler_params=params,
        cost_estimate=cost(1, 10),
        name="own",
    )(span_mask, section, section_gate, floor, queries, keys, values)

    for distance in range(1, spans):
        waiting = [(distance - 1, t) for t in turned] + [(distance, tuple(held))]
        forward = []
        for x in held:
            x, stat = lax.optimization_barrier((x, stat))
            forward.append(x)
        held = forward
        waiting[-1] = (distance, tuple(held))
        turned, held = travel(held, distance, turned)
        distances = [d for d, _ in waiting]

        blocks = [k for _, (k, _) in waiting] + [v for _, (_, v) in waiting]

        def step(*refs, distances=distances):
            step_kernel(distances, *refs)

        acc, stat = pl.pallas_call(
            step,
            out_shape=(acc_shape, stat_shape),
            in_specs=[VMEM] * (4 + len(blocks)),
            out_specs=(VMEM,) * 2,
            compiler_params=params,
            cost_estimate=cost(len(waiting)),
            name="step_%d" % distance,
        )(stacked, seen, acc, stat, *blocks)

    distances = [spans - 1] * len(turned)

    def close(*refs):
        close_kernel(distances, *refs)

    part, last_weight, log_total = pl.pallas_call(
        close,
        out_shape=(
            jax.ShapeDtypeStruct((kv_heads, width, HEAD_SIZE), jnp.float32),
            jax.ShapeDtypeStruct((kv_heads, width, len(turned) * rows), jnp.bfloat16),
            jax.ShapeDtypeStruct((heads, rows), jnp.float32),
        ),
        in_specs=[VMEM] * (5 + len(turned)),
        out_specs=(VMEM,) * 3,
        compiler_params=params,
        cost_estimate=cost(1),
        name="close",
    )(stacked, seen, gate_row, acc, stat, *[k for k, _ in turned])
    mixed = pl.pallas_call(
        mix_kernel,
        out_shape=jax.ShapeDtypeStruct((rows, wide), jnp.bfloat16),
        in_specs=[VMEM] * (3 + len(turned)),
        out_specs=HBM,
        scratch_shapes=[pltpu.VMEM((rows, wide), jnp.bfloat16), pltpu.SemaphoreType.DMA((kv_heads,))],
        compiler_params=params,
        cost_estimate=cost(1),
        name="mix",
    )(gate_row, part, last_weight, *[v for _, v in turned])
    return mixed, log_total


def solution(mesh):
    placed = (
        P(("grp", "tm"), "head"),
        P(("grp", "tm"), "head"),
        P(("grp", "tm"), "head"),
        P("grp", None),
        P("grp"),
        P(None, "head"),
    )
    return jax.shard_map(
        on_device,
        mesh=mesh,
        in_specs=placed,
        out_specs=(P(("grp", "tm"), "head"), P("head", ("grp", "tm"))),
        check_vma=False,
    )
```

```python
import math

import jax
import jax.numpy as jnp
from jax import lax
from jax.experimental import pallas as pl
from jax.experimental.pallas import tpu as pltpu
from jax.sharding import PartitionSpec as P

HEAD_SIZE = 128
CH = 256
LOG2E = math.log2(math.e)
FAR = 1e30
LIMIT = 2.0**80
SCALE = LOG2E / math.sqrt(HEAD_SIZE)
HBM = pl.BlockSpec(memory_space=pltpu.HBM)
VMEM = pl.BlockSpec(memory_space=pltpu.VMEM)


def head_columns(h):
    return slice(h * HEAD_SIZE, (h + 1) * HEAD_SIZE)


def against(queries, keys):
    return lax.dot_general(queries, keys, (((1,), (1,)), ((), ())), preferred_element_type=jnp.float32)


def with_ones(values):
    return jnp.concatenate([values, jnp.ones((values.shape[0], HEAD_SIZE), values.dtype)], axis=1)


def lanes(rows):
    return lax.broadcasted_iota(jnp.int32, (rows, HEAD_SIZE), 1)


def floor_kernel(floor):
    floor[...] = jnp.full(floor.shape, -FAR, jnp.float32)


def own_kernel(per_span, mask, section, gate, floor, q_hbm, k_hbm, v_hbm,
               stacked, tails, gate_row, tops, acc, q, k, v, sems):
    copies = [
        pltpu.make_async_copy(src, dst, sems.at[i])
        for i, (src, dst) in enumerate([(q_hbm, q), (k_hbm, k), (v_hbm, v)])
    ]
    for copy in copies:
        copy.start()
    span = lax.axis_index("tm") // per_span
    at = lanes(tails.shape[1])
    for distance in range(tails.shape[0]):
        allowed = jnp.logical_and(span >= distance, mask[span, jnp.maximum(span - distance, 0)] > 0)
        bias = jnp.where(allowed, 0.0, -FAR)
        tails[distance] = jnp.where(at < 3, 1.0, jnp.where(at == 3, bias, 0.0)).astype(jnp.bfloat16)
    gate_row[...] = gate[pl.ds(section[span], 1), :]
    for copy in copies:
        copy.wait()
    rows, width = q.shape[0], stacked.shape[1]
    group = width // rows
    every_top = jnp.zeros((rows, HEAD_SIZE), jnp.float32)
    at, beside = lanes(rows), lanes(width)
    for h in range(stacked.shape[0]):
        queries = jnp.concatenate([q[:, head_columns(h * group + g)] for g in range(group)], axis=0)
        score = against(queries, k[:, head_columns(h)])
        top = jnp.maximum(floor[0:1, 0:1], jnp.max(score, axis=1, keepdims=True))
        weight = jnp.exp2(SCALE * (score - top)).astype(jnp.bfloat16)
        acc[h] = jnp.dot(weight, with_ones(v[:, head_columns(h)]), preferred_element_type=jnp.float32)
        high = top.astype(jnp.bfloat16).astype(jnp.float32)
        middle = (top - high).astype(jnp.bfloat16).astype(jnp.float32)
        low = top - high - middle
        extra = jnp.where(
            beside == 0, -high, jnp.where(beside == 1, -middle, jnp.where(beside == 2, -low, jnp.where(beside == 3, 1.0, 0.0)))
        )
        stacked[h] = jnp.concatenate([queries, extra.astype(jnp.bfloat16)], axis=1)
        for g in range(group):
            every_top = jnp.where(at == h * group + g, top[g * rows : (g + 1) * rows, :], every_top)
    tops[...] = every_top.T[: tops.shape[0], :] * (1.0 / math.sqrt(HEAD_SIZE))


def weights_of(h, distances, stacked, tails, key_refs):
    keys = jnp.concatenate(
        [jnp.concatenate([k[:, head_columns(h)], tails[d]], axis=1) for d, k in zip(distances, key_refs)], axis=0
    )
    return jnp.exp2(SCALE * against(stacked[h], keys))


def step_kernel(distances, stacked, tails, acc_in, *refs):
    count = len(distances)
    key_refs, value_refs, (acc,) = refs[:count], refs[count : 2 * count], refs[2 * count :]
    for h in range(stacked.shape[0]):
        weight = weights_of(h, distances, stacked, tails, key_refs).astype(jnp.bfloat16)
        values = with_ones(jnp.concatenate([v[:, head_columns(h)] for v in value_refs], axis=0))
        acc[h] = acc_in[h] + jnp.dot(weight, values, preferred_element_type=jnp.float32)


def close_kernel(distances, last, stacked, tails, gate_row, tops, acc, *refs):
    count = len(distances)
    key_refs, value_refs, (part, last_weight, log_ref) = refs[:count], refs[count : 2 * count - last], refs[2 * count - last :]
    heads, rows = log_ref.shape
    width = stacked.shape[1]
    group = width // rows
    at = lanes(rows)

    def gated(h, g, attended):
        columns = pl.ds(pl.multiple_of((h * group + g) * HEAD_SIZE, HEAD_SIZE), HEAD_SIZE)
        part[h, g * rows : (g + 1) * rows, :] = attended[g * rows : (g + 1) * rows, :] * gate_row[:, columns]

    every_total = jnp.ones((rows, HEAD_SIZE), jnp.float32)
    for h in range(stacked.shape[0]):
        weight = weights_of(h, distances[-last:], stacked, tails, key_refs[-last:])
        ones = jnp.ones((weight.shape[1], HEAD_SIZE), jnp.bfloat16)
        total = acc[h, :, HEAD_SIZE:] + jnp.dot(weight.astype(jnp.bfloat16), ones, preferred_element_type=jnp.float32)
        inverse = 1.0 / total
        for i in range(last):
            last_weight[h, :, head_columns(i)] = (weight[:, head_columns(i)] * inverse).astype(jnp.bfloat16)
        attended = acc[h, :, :HEAD_SIZE] * inverse
        for g in range(group):
            gated(h, g, attended)
            every_total = jnp.where(at == h * group + g, total[g * rows : (g + 1) * rows, :], every_total)
    log_ref[...] = tops[...] + jnp.log(every_total.T[:heads, :])
    outside = jnp.max(jnp.where(every_total <= LIMIT, 0.0, 1.0))

    @pl.when(outside > 0.0)
    def _():
        def one_head(h, carry):
            every_top, every_total = carry
            inside = pl.ds(pl.multiple_of(h * HEAD_SIZE, HEAD_SIZE), HEAD_SIZE)
            queries = stacked[h, :, :HEAD_SIZE]
            bias = [tails[d, 0:1, 3:4].astype(jnp.float32) for d in distances]
            top = None
            for k, b in zip(key_refs, bias):
                row = jnp.max(against(queries, k[:, inside]) + b, axis=1, keepdims=True)
                top = row if top is None else jnp.maximum(top, row)
            total = jnp.zeros((width, 1), jnp.float32)
            attended = jnp.zeros((width, HEAD_SIZE), jnp.float32)
            late = []
            for i, (k, b) in enumerate(zip(key_refs, bias)):
                weight = jnp.exp2(SCALE * (against(queries, k[:, inside]) + b - top))
                total += jnp.sum(weight, axis=1, keepdims=True)
                if i < count - last:
                    attended += jnp.dot(
                        weight.astype(jnp.bfloat16), value_refs[i][:, inside], preferred_element_type=jnp.float32
                    )
                else:
                    late.append(weight)
            inverse = 1.0 / total
            for i, weight in enumerate(late):
                last_weight[h, :, head_columns(i)] = (weight * inverse).astype(jnp.bfloat16)
            attended = attended * inverse
            for g in range(group):
                gated(h, g, attended)
                here = at == h * group + g
                every_top = jnp.where(here, top[g * rows : (g + 1) * rows, :], every_top)
                every_total = jnp.where(here, total[g * rows : (g + 1) * rows, :], every_total)
            return every_top, every_total

        start = (jnp.zeros((rows, HEAD_SIZE), jnp.float32), jnp.ones((rows, HEAD_SIZE), jnp.float32))
        every_top, every_total = lax.fori_loop(0, stacked.shape[0], one_head, start)
        log_ref[...] = (every_top.T * (1.0 / math.sqrt(HEAD_SIZE)) + jnp.log(every_total.T))[:heads, :]


def mix_kernel(gate_row, part, last_weight, *refs):
    value_refs, (mixed_hbm, mixed, sems) = refs[:-3], refs[-3:]
    kv_heads, width = part.shape[0], part.shape[1]
    rows = mixed.shape[0]
    group = width // rows
    copies = []
    for h in range(kv_heads):
        values = jnp.concatenate([v[:, head_columns(h)] for v in value_refs], axis=0)
        rest = jnp.dot(last_weight[h], values, preferred_element_type=jnp.float32)
        for g in range(group):
            inside = slice(g * rows, (g + 1) * rows)
            columns = head_columns(h * group + g)
            mixed[:, columns] = (part[h, inside, :] + gate_row[:, columns] * rest[inside, :]).astype(jnp.bfloat16)
        columns = pl.ds(h * group * HEAD_SIZE, group * HEAD_SIZE)
        copies.append(pltpu.make_async_copy(mixed.at[:, columns], mixed_hbm.at[:, columns], sems.at[h]))
        copies[-1].start()
    for copy in copies:
        copy.wait()


def on_device(queries, keys, values, span_mask, section, section_gate):
    rows, wide = queries.shape
    heads, kv_heads = wide // HEAD_SIZE, keys.shape[1] // HEAD_SIZE
    width = heads // kv_heads * rows
    count = lax.axis_size("tm")
    per_span = CH // rows
    spans = count // per_span
    params = pltpu.CompilerParams(vmem_limit_bytes=24 * 1024 * 1024)
    acc_shape = jax.ShapeDtypeStruct((kv_heads, width, 2 * HEAD_SIZE), jnp.float32)

    def cost(blocks, times=2):
        return pl.CostEstimate(
            flops=4 * times * blocks * rows * rows * wide, bytes_accessed=rows * wide * 8, transcendentals=blocks * rows * rows * heads
        )

    cores = lax.axis_size("head")

    def send(value, target):
        pairs = []
        for i in range(count):
            for core in range(cores):
                if target(i) is None:
                    goal = i * cores + (core + 1) % cores if cores > 1 else i
                else:
                    goal = target(i) * cores + core
                pairs.append((i * cores + core, goal))
        return lax.ppermute(value, ("tm", "head"), pairs)

    def onward(value, distance):
        first = (distance - 1) * per_span

        def target(i):
            if i < first:
                return None
            return i + per_span if i + per_span < count else first + i % per_span

        return send(value, target)

    def around(value, distance, turn):
        return send(
            value, lambda i: i - i % per_span + (i + turn) % per_span if i >= distance * per_span else None
        )

    def travel(held, distance, turned_before):
        onwards = [onward(x, distance + 1) for x in held] if distance + 1 < spans else []
        turned = [[around(x, distance, turn) for turn in range(1, per_span)] for x in held]
        if not onwards and turned_before:
            turned[1] = [onward(v, distance) for _, v in turned_before]
        return list(zip(*turned)), onwards

    floor = pl.pallas_call(
        floor_kernel,
        out_shape=jax.ShapeDtypeStruct((8, width), jnp.float32),
        out_specs=VMEM,
        compiler_params=params,
        cost_estimate=cost(4, 10),
        name="floor",
    )()
    held = [onward(x, 1) for x in (keys, values)] if spans > 1 else []
    near_keys, near_values, floor = lax.optimization_barrier((keys, values, floor))
    turned = list(zip(*[[around(x, 0, turn) for turn in range(1, per_span)] for x in (near_keys, near_values)]))
    def own(*refs):
        own_kernel(per_span, *refs)

    stacked, tails, gate_row, tops, acc = pl.pallas_call(
        own,
        out_shape=(
            jax.ShapeDtypeStruct((kv_heads, width, 2 * HEAD_SIZE), jnp.bfloat16),
            jax.ShapeDtypeStruct((spans, rows, HEAD_SIZE), jnp.bfloat16),
            jax.ShapeDtypeStruct((1, wide), jnp.float32),
            jax.ShapeDtypeStruct((heads, rows), jnp.float32),
            acc_shape,
        ),
        in_specs=[pl.BlockSpec(memory_space=pltpu.SMEM)] * 2 + [VMEM] * 2 + [HBM] * 3,
        out_specs=(VMEM,) * 5,
        scratch_shapes=[
            pltpu.VMEM(queries.shape, queries.dtype),
            pltpu.VMEM(keys.shape, keys.dtype),
            pltpu.VMEM(values.shape, values.dtype),
            pltpu.SemaphoreType.DMA((3,)),
        ],
        compiler_params=params,
        cost_estimate=cost(1, 10),
        name="own",
    )(span_mask, section, section_gate, floor, queries, keys, values)

    seen_blocks = [(0, (keys, values))]
    for distance in range(1, spans):
        waiting = [(distance - 1, t) for t in turned]
        forward = []
        for x in held:
            x, acc = lax.optimization_barrier((x, acc))
            forward.append(x)
        held = forward
        waiting.append((distance, tuple(held)))
        turned, held = travel(held, distance, turned)
        distances = [d for d, _ in waiting]
        blocks = [k for _, (k, _) in waiting] + [v for _, (_, v) in waiting]
        seen_blocks += waiting

        def step(*refs, distances=distances):
            step_kernel(distances, *refs)

        acc = pl.pallas_call(
            step,
            out_shape=acc_shape,
            in_specs=[VMEM] * (3 + len(blocks)),
            out_specs=VMEM,
            compiler_params=params,
            cost_estimate=cost(len(waiting)),
            name="step_%d" % distance,
        )(stacked, tails, acc, *blocks)

    distances = [d for d, _ in seen_blocks] + [spans - 1] * len(turned)

    def close(*refs):
        close_kernel(distances, len(turned), *refs)

    blocks = [k for _, (k, _) in seen_blocks] + [k for k, _ in turned] + [v for _, (_, v) in seen_blocks]
    part, last_weight, log_total = pl.pallas_call(
        close,
        out_shape=(
            jax.ShapeDtypeStruct((kv_heads, width, HEAD_SIZE), jnp.float32),
            jax.ShapeDtypeStruct((kv_heads, width, len(turned) * rows), jnp.bfloat16),
            jax.ShapeDtypeStruct((heads, rows), jnp.float32),
        ),
        in_specs=[VMEM] * (5 + len(blocks)),
        out_specs=(VMEM,) * 3,
        compiler_params=params,
        cost_estimate=cost(1),
        name="close",
    )(stacked, tails, gate_row, tops, acc, *blocks)
    mixed = pl.pallas_call(
        mix_kernel,
        out_shape=jax.ShapeDtypeStruct((rows, wide), jnp.bfloat16),
        in_specs=[VMEM] * (3 + len(turned)),
        out_specs=HBM,
        scratch_shapes=[pltpu.VMEM((rows, wide), jnp.bfloat16), pltpu.SemaphoreType.DMA((kv_heads,))],
        compiler_params=params,
        cost_estimate=cost(1),
        name="mix",
    )(gate_row, part, last_weight, *[v for _, v in turned])
    return mixed, log_total


def solution(mesh):
    placed = (
        P(("grp", "tm"), "head"),
        P(("grp", "tm"), "head"),
        P(("grp", "tm"), "head"),
        P("grp", None),
        P("grp"),
        P(None, "head"),
    )
    return jax.shard_map(
        on_device,
        mesh=mesh,
        in_specs=placed,
        out_specs=(P(("grp", "tm"), "head"), P("head", ("grp", "tm"))),
        check_vma=False,
    )
```

```python
import math

import jax
import jax.numpy as jnp
from jax import lax
from jax.experimental import pallas as pl
from jax.experimental.pallas import tpu as pltpu
from jax.sharding import PartitionSpec as P

HEAD_SIZE = 128
CH = 256
LOG2E = math.log2(math.e)
FAR = 1e30
LIMIT = 2.0**80
SCALE = LOG2E / math.sqrt(HEAD_SIZE)
HBM = pl.BlockSpec(memory_space=pltpu.HBM)
VMEM = pl.BlockSpec(memory_space=pltpu.VMEM)


def head_columns(h):
    return slice(h * HEAD_SIZE, (h + 1) * HEAD_SIZE)


def against(queries, keys):
    return lax.dot_general(queries, keys, (((1,), (1,)), ((), ())), preferred_element_type=jnp.float32)


def with_ones(values):
    return jnp.concatenate([values, jnp.ones((values.shape[0], HEAD_SIZE), values.dtype)], axis=1)


def lanes(rows):
    return lax.broadcasted_iota(jnp.int32, (rows, HEAD_SIZE), 1)


def floor_kernel(floor):
    floor[...] = jnp.full(floor.shape, -FAR, jnp.float32)


def own_kernel(per_span, mask, section, gate, floor, q_hbm, k_hbm, v_hbm,
               stacked, tails, gate_row, tops, acc, q, k, v, sems):
    copies = [
        pltpu.make_async_copy(src, dst, sems.at[i])
        for i, (src, dst) in enumerate([(q_hbm, q), (k_hbm, k), (v_hbm, v)])
    ]
    for copy in copies:
        copy.start()
    span = lax.axis_index("tm") // per_span
    at = lanes(tails.shape[1])
    for distance in range(tails.shape[0]):
        allowed = jnp.logical_and(span >= distance, mask[span, jnp.maximum(span - distance, 0)] > 0)
        bias = jnp.where(allowed, 0.0, -FAR)
        tails[distance] = jnp.where(at < 3, 1.0, jnp.where(at == 3, bias, 0.0)).astype(jnp.bfloat16)
    gate_row[...] = gate[pl.ds(section[span], 1), :]
    for copy in copies:
        copy.wait()
    rows, width = q.shape[0], stacked.shape[1]
    group = width // rows
    at = lanes(1)
    for h in range(stacked.shape[0]):
        queries = jnp.concatenate([q[:, head_columns(h * group + g)] for g in range(group)], axis=0)
        score = against(queries, k[:, head_columns(h)])
        top = jnp.maximum(floor[0:1, 0:1], jnp.max(jnp.max(score, axis=0, keepdims=True), axis=1, keepdims=True))
        weight = jnp.exp2(SCALE * (score - top)).astype(jnp.bfloat16)
        acc[h] = jnp.dot(weight, with_ones(v[:, head_columns(h)]), preferred_element_type=jnp.float32)
        high = top.astype(jnp.bfloat16).astype(jnp.float32)
        middle = (top - high).astype(jnp.bfloat16).astype(jnp.float32)
        low = top - high - middle
        extra = jnp.where(at == 0, -high, jnp.where(at == 1, -middle, jnp.where(at == 2, -low, jnp.where(at == 3, 1.0, 0.0))))
        extra = jnp.broadcast_to(extra, (width, HEAD_SIZE)).astype(jnp.bfloat16)
        stacked[h] = jnp.concatenate([queries, extra], axis=1)
        tops[h * group : (h + 1) * group, :] = jnp.broadcast_to(top * (1.0 / math.sqrt(HEAD_SIZE)), (group, rows))


def weights_of(h, distances, stacked, tails, key_refs):
    keys = jnp.concatenate(
        [jnp.concatenate([k[:, head_columns(h)], tails[d]], axis=1) for d, k in zip(distances, key_refs)], axis=0
    )
    return jnp.exp2(SCALE * against(stacked[h], keys))


def step_kernel(distances, stacked, tails, acc_in, *refs):
    count = len(distances)
    key_refs, value_refs, (acc,) = refs[:count], refs[count : 2 * count], refs[2 * count :]
    for h in range(stacked.shape[0]):
        weight = weights_of(h, distances, stacked, tails, key_refs).astype(jnp.bfloat16)
        values = with_ones(jnp.concatenate([v[:, head_columns(h)] for v in value_refs], axis=0))
        acc[h] = acc_in[h] + jnp.dot(weight, values, preferred_element_type=jnp.float32)


def close_kernel(distances, last, stacked, tails, gate_row, tops, acc, *refs):
    count = len(distances)
    key_refs, value_refs, (part, last_weight, log_ref) = refs[:count], refs[count : 2 * count - last], refs[2 * count - last :]
    heads, rows = log_ref.shape
    width = stacked.shape[1]
    group = width // rows
    at = lanes(rows)

    def gated(h, g, attended):
        columns = pl.ds(pl.multiple_of((h * group + g) * HEAD_SIZE, HEAD_SIZE), HEAD_SIZE)
        part[h, g * rows : (g + 1) * rows, :] = attended[g * rows : (g + 1) * rows, :] * gate_row[:, columns]

    every_total = jnp.ones((rows, HEAD_SIZE), jnp.float32)
    for h in range(stacked.shape[0]):
        weight = weights_of(h, distances[-last:], stacked, tails, key_refs[-last:])
        ones = jnp.ones((weight.shape[1], HEAD_SIZE), jnp.bfloat16)
        total = acc[h, :, HEAD_SIZE:] + jnp.dot(weight.astype(jnp.bfloat16), ones, preferred_element_type=jnp.float32)
        inverse = pl.reciprocal(total, approx=True)
        inverse = inverse * (2.0 - total * inverse)
        for i in range(last):
            last_weight[h, :, head_columns(i)] = (weight[:, head_columns(i)] * inverse).astype(jnp.bfloat16)
        attended = acc[h, :, :HEAD_SIZE] * inverse
        for g in range(group):
            gated(h, g, attended)
            every_total = jnp.where(at == h * group + g, total[g * rows : (g + 1) * rows, :], every_total)
    log_ref[...] = tops[...] + jnp.log(every_total.T[:heads, :])
    fits = jnp.logical_and(every_total <= LIMIT, every_total >= 1.0 / LIMIT)
    outside = jnp.max(jnp.where(fits, 0.0, 1.0))

    @pl.when(outside > 0.0)
    def _():
        def one_head(h, carry):
            every_top, every_total = carry
            inside = pl.ds(pl.multiple_of(h * HEAD_SIZE, HEAD_SIZE), HEAD_SIZE)
            queries = stacked[h, :, :HEAD_SIZE]
            bias = [tails[d, 0:1, 3:4].astype(jnp.float32) for d in distances]
            top = None
            for k, b in zip(key_refs, bias):
                row = jnp.max(against(queries, k[:, inside]) + b, axis=1, keepdims=True)
                top = row if top is None else jnp.maximum(top, row)
            total = jnp.zeros((width, 1), jnp.float32)
            attended = jnp.zeros((width, HEAD_SIZE), jnp.float32)
            late = []
            for i, (k, b) in enumerate(zip(key_refs, bias)):
                weight = jnp.exp2(SCALE * (against(queries, k[:, inside]) + b - top))
                total += jnp.sum(weight, axis=1, keepdims=True)
                if i < count - last:
                    attended += jnp.dot(
                        weight.astype(jnp.bfloat16), value_refs[i][:, inside], preferred_element_type=jnp.float32
                    )
                else:
                    late.append(weight)
            inverse = 1.0 / total
            for i, weight in enumerate(late):
                last_weight[h, :, head_columns(i)] = (weight * inverse).astype(jnp.bfloat16)
            attended = attended * inverse
            for g in range(group):
                gated(h, g, attended)
                here = at == h * group + g
                every_top = jnp.where(here, top[g * rows : (g + 1) * rows, :], every_top)
                every_total = jnp.where(here, total[g * rows : (g + 1) * rows, :], every_total)
            return every_top, every_total

        start = (jnp.zeros((rows, HEAD_SIZE), jnp.float32), jnp.ones((rows, HEAD_SIZE), jnp.float32))
        every_top, every_total = lax.fori_loop(0, stacked.shape[0], one_head, start)
        log_ref[...] = (every_top.T * (1.0 / math.sqrt(HEAD_SIZE)) + jnp.log(every_total.T))[:heads, :]


def mix_kernel(gate_row, part, last_weight, *refs):
    value_refs, (mixed_hbm, mixed, sems) = refs[:-3], refs[-3:]
    kv_heads, width = part.shape[0], part.shape[1]
    rows = mixed.shape[0]
    group = width // rows
    copies = []
    for h in range(kv_heads):
        values = jnp.concatenate([v[:, head_columns(h)] for v in value_refs], axis=0)
        rest = jnp.dot(last_weight[h], values, preferred_element_type=jnp.float32)
        for g in range(group):
            inside = slice(g * rows, (g + 1) * rows)
            columns = head_columns(h * group + g)
            mixed[:, columns] = (part[h, inside, :] + gate_row[:, columns] * rest[inside, :]).astype(jnp.bfloat16)
        columns = pl.ds(h * group * HEAD_SIZE, group * HEAD_SIZE)
        copies.append(pltpu.make_async_copy(mixed.at[:, columns], mixed_hbm.at[:, columns], sems.at[h]))
        copies[-1].start()
    for copy in copies:
        copy.wait()


def on_device(queries, keys, values, span_mask, section, section_gate):
    rows, wide = queries.shape
    heads, kv_heads = wide // HEAD_SIZE, keys.shape[1] // HEAD_SIZE
    width = heads // kv_heads * rows
    count = lax.axis_size("tm")
    per_span = CH // rows
    spans = count // per_span
    params = pltpu.CompilerParams(vmem_limit_bytes=24 * 1024 * 1024)
    acc_shape = jax.ShapeDtypeStruct((kv_heads, width, 2 * HEAD_SIZE), jnp.float32)

    def cost(blocks, times=2):
        return pl.CostEstimate(
            flops=4 * times * blocks * rows * rows * wide, bytes_accessed=rows * wide * 8, transcendentals=blocks * rows * rows * heads
        )

    cores, clips = lax.axis_size("head"), lax.axis_size("grp")

    def send(value, target):
        pairs = []
        for clip in range(clips):
            for i in range(count):
                for core in range(cores):
                    goal = (clip, target(i), core)
                    if target(i) is None:
                        goal = ((clip + 1) % clips, i, core if clips > 1 else (core + 1) % cores)
                    pairs.append(tuple((c * count + j) * cores + k for c, j, k in ((clip, i, core), goal)))
        return lax.ppermute(value, ("grp", "tm", "head"), pairs)

    def onward(value, distance):
        first = (distance - 1) * per_span

        def target(i):
            if i < first:
                return None
            return i + per_span if i + per_span < count else first + i % per_span

        return send(value, target)

    def around(value, distance, turn):
        return send(
            value, lambda i: i - i % per_span + (i + turn) % per_span if i >= distance * per_span else None
        )

    def leap(value):
        far = (spans - 1) * per_span

        def target(i):
            return i + far if i < per_span else i - far if i >= far else None

        return send(value, target)

    def exchange(held, distance):
        return list(zip(*[[around(x, distance, turn) for turn in range(1, per_span)] for x in held]))

    floor = pl.pallas_call(
        floor_kernel,
        out_shape=jax.ShapeDtypeStruct((8, width), jnp.float32),
        out_specs=VMEM,
        compiler_params=params,
        cost_estimate=cost(4, 10),
        name="floor",
    )()
    held = [onward(x, 1) for x in (keys, values)] if spans > 2 else []
    near_keys, near_values, floor = lax.optimization_barrier((keys, values, floor))
    turned = exchange((near_keys, near_values), 0)
    beside_keys = [k for k, _ in turned]
    def own(*refs):
        own_kernel(per_span, *refs)

    stacked, tails, gate_row, tops, acc = pl.pallas_call(
        own,
        out_shape=(
            jax.ShapeDtypeStruct((kv_heads, width, 2 * HEAD_SIZE), jnp.bfloat16),
            jax.ShapeDtypeStruct((spans, rows, HEAD_SIZE), jnp.bfloat16),
            jax.ShapeDtypeStruct((1, wide), jnp.float32),
            jax.ShapeDtypeStruct((heads, rows), jnp.float32),
            acc_shape,
        ),
        in_specs=[pl.BlockSpec(memory_space=pltpu.SMEM)] * 2 + [VMEM] * 2 + [HBM] * 3,
        out_specs=(VMEM,) * 5,
        scratch_shapes=[
            pltpu.VMEM(queries.shape, queries.dtype),
            pltpu.VMEM(keys.shape, keys.dtype),
            pltpu.VMEM(values.shape, values.dtype),
            pltpu.SemaphoreType.DMA((3,)),
        ],
        compiler_params=params,
        cost_estimate=cost(1, 10),
        name="own",
    )(span_mask, section, section_gate, floor, queries, keys, values)

    seen_blocks = [(0, (keys, values))]

    def advance(acc, blocks):
        seen_blocks.extend(blocks)
        operands = [k for _, (k, _) in blocks] + [v for _, (_, v) in blocks]

        def step(*refs):
            step_kernel([d for d, _ in blocks], *refs)

        return pl.pallas_call(
            step,
            out_shape=acc_shape,
            in_specs=[VMEM] * (3 + len(operands)),
            out_specs=VMEM,
            compiler_params=params,
            cost_estimate=cost(len(blocks)),
            name="step_%d" % blocks[-1][0],
        )(stacked, tails, acc, *operands)

    def far_sends(acc):
        sent = []
        for x in [keys, values] + beside_keys:
            x, acc = lax.optimization_barrier((x, acc))
            sent.append(leap(x))
        return acc, sent[:2], sent[2:]

    far_held = None
    for distance in range(1, spans - 1):
        waiting = [(distance - 1, t) for t in turned]
        forward = []
        for x in held:
            x, acc = lax.optimization_barrier((x, acc))
            forward.append(x)
        waiting.append((distance, tuple(forward)))
        held = [onward(x, distance + 1) for x in forward] if distance + 2 < spans else []
        turned = exchange(forward, distance)
        acc = advance(acc, waiting)
        if far_held is None:
            acc, far_held, far_keys = far_sends(acc)
    last_blocks = [(max(spans - 2, 0), t) for t in turned]
    if spans > 1:
        if far_held is None:
            acc, far_held, far_keys = far_sends(acc)
        far_values = [around(far_held[1], spans - 1, turn) for turn in range(1, per_span)]
        acc = advance(acc, [(spans - 1, tuple(far_held))])
        last_blocks += [(spans - 1, t) for t in zip(far_keys, far_values)]

    distances = [d for d, _ in seen_blocks + last_blocks]

    def close(*refs):
        close_kernel(distances, len(last_blocks), *refs)

    blocks = [k for _, (k, _) in seen_blocks + last_blocks] + [v for _, (_, v) in seen_blocks]
    part, last_weight, log_total = pl.pallas_call(
        close,
        out_shape=(
            jax.ShapeDtypeStruct((kv_heads, width, HEAD_SIZE), jnp.float32),
            jax.ShapeDtypeStruct((kv_heads, width, len(last_blocks) * rows), jnp.bfloat16),
            jax.ShapeDtypeStruct((heads, rows), jnp.float32),
        ),
        in_specs=[VMEM] * (5 + len(blocks)),
        out_specs=(VMEM,) * 3,
        compiler_params=params,
        cost_estimate=cost(1),
        name="close",
    )(stacked, tails, gate_row, tops, acc, *blocks)
    mixed = pl.pallas_call(
        mix_kernel,
        out_shape=jax.ShapeDtypeStruct((rows, wide), jnp.bfloat16),
        in_specs=[VMEM] * (3 + len(last_blocks)),
        out_specs=HBM,
        scratch_shapes=[pltpu.VMEM((rows, wide), jnp.bfloat16), pltpu.SemaphoreType.DMA((kv_heads,))],
        compiler_params=params,
        cost_estimate=cost(1),
        name="mix",
    )(gate_row, part, last_weight, *[v for _, (_, v) in last_blocks])
    return mixed, log_total


def solution(mesh):
    placed = (
        P(("grp", "tm"), "head"),
        P(("grp", "tm"), "head"),
        P(("grp", "tm"), "head"),
        P("grp", None),
        P("grp"),
        P(None, "head"),
    )
    return jax.shard_map(
        on_device,
        mesh=mesh,
        in_specs=placed,
        out_specs=(P(("grp", "tm"), "head"), P("head", ("grp", "tm"))),
        check_vma=False,
    )
```

```python
import math

import jax
import jax.numpy as jnp
from jax import lax
from jax.experimental import pallas as pl
from jax.experimental.pallas import tpu as pltpu
from jax.sharding import PartitionSpec as P

HEAD_SIZE = 128
CH = 256
LOG2E = math.log2(math.e)
FAR = 1e30
LIMIT = 2.0**80
SCALE = LOG2E / math.sqrt(HEAD_SIZE)
HBM = pl.BlockSpec(memory_space=pltpu.HBM)
VMEM = pl.BlockSpec(memory_space=pltpu.VMEM)


def head_columns(h):
    return slice(h * HEAD_SIZE, (h + 1) * HEAD_SIZE)


def against(queries, keys):
    return lax.dot_general(queries, keys, (((1,), (1,)), ((), ())), preferred_element_type=jnp.float32)


def with_ones(values):
    return jnp.concatenate([values, jnp.ones((values.shape[0], HEAD_SIZE), values.dtype)], axis=1)


def lanes(rows):
    return lax.broadcasted_iota(jnp.int32, (rows, HEAD_SIZE), 1)


def floor_kernel(floor):
    floor[...] = jnp.full(floor.shape, -FAR, jnp.float32)


def prepare_kernel(per_span, mask, section, gate, floor, q_hbm, k_hbm, stacked, tails, gate_row, tops, q, k, sems):
    copies = [
        pltpu.make_async_copy(src, dst, sems.at[i])
        for i, (src, dst) in enumerate([(q_hbm, q), (k_hbm, k)])
    ]
    for copy in copies:
        copy.start()
    span = lax.axis_index("tm") // per_span
    at = lanes(tails.shape[1])
    for distance in range(tails.shape[0]):
        allowed = jnp.logical_and(span >= distance, mask[span, jnp.maximum(span - distance, 0)] > 0)
        bias = jnp.where(allowed, 0.0, -FAR)
        tails[distance] = jnp.where(at < 3, 1.0, jnp.where(at == 3, bias, 0.0)).astype(jnp.bfloat16)
    gate_row[...] = gate[pl.ds(section[span], 1), :]
    for copy in copies:
        copy.wait()
    rows, width = q.shape[0], stacked.shape[1]
    group = width // rows
    at = lanes(1)
    for h in range(stacked.shape[0]):
        queries = jnp.concatenate([q[:, head_columns(h * group + g)] for g in range(group)], axis=0)
        score = against(queries, k[:, head_columns(h)])
        top = jnp.maximum(floor[0:1, 0:1], jnp.max(jnp.max(score, axis=0, keepdims=True), axis=1, keepdims=True))
        high = top.astype(jnp.bfloat16).astype(jnp.float32)
        middle = (top - high).astype(jnp.bfloat16).astype(jnp.float32)
        low = top - high - middle
        extra = jnp.where(at == 0, -high, jnp.where(at == 1, -middle, jnp.where(at == 2, -low, jnp.where(at == 3, 1.0, 0.0))))
        extra = jnp.broadcast_to(extra, (width, HEAD_SIZE)).astype(jnp.bfloat16)
        stacked[h] = jnp.concatenate([queries, extra], axis=1)
        tops[h * group : (h + 1) * group, :] = jnp.broadcast_to(top * (1.0 / math.sqrt(HEAD_SIZE)), (group, rows))


def weights_of(h, distances, stacked, tails, key_refs):
    keys = jnp.concatenate(
        [jnp.concatenate([k[:, head_columns(h)], tails[d]], axis=1) for d, k in zip(distances, key_refs)], axis=0
    )
    return jnp.exp2(SCALE * against(stacked[h], keys))


def step_kernel(distances, first, stacked, tails, *refs):
    count = len(distances)
    acc_in = None if first else refs[0]
    refs = refs[0 if first else 1 :]
    key_refs, value_refs, (acc,) = refs[:count], refs[count : 2 * count], refs[2 * count :]
    for h in range(stacked.shape[0]):
        weight = weights_of(h, distances, stacked, tails, key_refs).astype(jnp.bfloat16)
        values = with_ones(jnp.concatenate([v[:, head_columns(h)] for v in value_refs], axis=0))
        attended = jnp.dot(weight, values, preferred_element_type=jnp.float32)
        acc[h] = attended if first else acc_in[h] + attended


def close_kernel(distances, last, stacked, tails, gate_row, tops, acc, *refs):
    count = len(distances)
    key_refs, value_refs, (part, last_weight, log_ref) = refs[:count], refs[count : 2 * count - last], refs[2 * count - last :]
    heads, rows = log_ref.shape
    width = stacked.shape[1]
    group = width // rows
    at = lanes(rows)

    def gated(h, g, attended):
        columns = pl.ds(pl.multiple_of((h * group + g) * HEAD_SIZE, HEAD_SIZE), HEAD_SIZE)
        part[h, g * rows : (g + 1) * rows, :] = attended[g * rows : (g + 1) * rows, :] * gate_row[:, columns]

    every_total = jnp.ones((rows, HEAD_SIZE), jnp.float32)
    for h in range(stacked.shape[0]):
        weight = weights_of(h, distances[-last:], stacked, tails, key_refs[-last:])
        ones = jnp.ones((weight.shape[1], HEAD_SIZE), jnp.bfloat16)
        total = acc[h, :, HEAD_SIZE:] + jnp.dot(weight.astype(jnp.bfloat16), ones, preferred_element_type=jnp.float32)
        inverse = pl.reciprocal(total, approx=True)
        inverse = inverse * (2.0 - total * inverse)
        for i in range(last):
            last_weight[h, :, head_columns(i)] = (weight[:, head_columns(i)] * inverse).astype(jnp.bfloat16)
        attended = acc[h, :, :HEAD_SIZE] * inverse
        for g in range(group):
            gated(h, g, attended)
            every_total = jnp.where(at == h * group + g, total[g * rows : (g + 1) * rows, :], every_total)
    log_ref[...] = tops[...] + jnp.log(every_total.T[:heads, :])
    fits = jnp.logical_and(every_total <= LIMIT, every_total >= 1.0 / LIMIT)
    outside = jnp.max(jnp.where(fits, 0.0, 1.0))

    @pl.when(outside > 0.0)
    def _():
        def one_head(h, carry):
            every_top, every_total = carry
            inside = pl.ds(pl.multiple_of(h * HEAD_SIZE, HEAD_SIZE), HEAD_SIZE)
            queries = stacked[h, :, :HEAD_SIZE]
            bias = [tails[d, 0:1, 3:4].astype(jnp.float32) for d in distances]
            top = None
            for k, b in zip(key_refs, bias):
                row = jnp.max(against(queries, k[:, inside]) + b, axis=1, keepdims=True)
                top = row if top is None else jnp.maximum(top, row)
            total = jnp.zeros((width, 1), jnp.float32)
            attended = jnp.zeros((width, HEAD_SIZE), jnp.float32)
            late = []
            for i, (k, b) in enumerate(zip(key_refs, bias)):
                weight = jnp.exp2(SCALE * (against(queries, k[:, inside]) + b - top))
                total += jnp.sum(weight, axis=1, keepdims=True)
                if i < count - last:
                    attended += jnp.dot(
                        weight.astype(jnp.bfloat16), value_refs[i][:, inside], preferred_element_type=jnp.float32
                    )
                else:
                    late.append(weight)
            inverse = 1.0 / total
            for i, weight in enumerate(late):
                last_weight[h, :, head_columns(i)] = (weight * inverse).astype(jnp.bfloat16)
            attended = attended * inverse
            for g in range(group):
                gated(h, g, attended)
                here = at == h * group + g
                every_top = jnp.where(here, top[g * rows : (g + 1) * rows, :], every_top)
                every_total = jnp.where(here, total[g * rows : (g + 1) * rows, :], every_total)
            return every_top, every_total

        start = (jnp.zeros((rows, HEAD_SIZE), jnp.float32), jnp.ones((rows, HEAD_SIZE), jnp.float32))
        every_top, every_total = lax.fori_loop(0, stacked.shape[0], one_head, start)
        log_ref[...] = (every_top.T * (1.0 / math.sqrt(HEAD_SIZE)) + jnp.log(every_total.T))[:heads, :]


def mix_kernel(gate_row, part, last_weight, *refs):
    value_refs, (mixed_hbm, mixed, sems) = refs[:-3], refs[-3:]
    kv_heads, width = part.shape[0], part.shape[1]
    rows = mixed.shape[0]
    group = width // rows
    copies = []
    for h in range(kv_heads):
        values = jnp.concatenate([v[:, head_columns(h)] for v in value_refs], axis=0)
        rest = jnp.dot(last_weight[h], values, preferred_element_type=jnp.float32)
        for g in range(group):
            inside = slice(g * rows, (g + 1) * rows)
            columns = head_columns(h * group + g)
            mixed[:, columns] = (part[h, inside, :] + gate_row[:, columns] * rest[inside, :]).astype(jnp.bfloat16)
        columns = pl.ds(h * group * HEAD_SIZE, group * HEAD_SIZE)
        copies.append(pltpu.make_async_copy(mixed.at[:, columns], mixed_hbm.at[:, columns], sems.at[h]))
        copies[-1].start()
    for copy in copies:
        copy.wait()


def on_device(queries, keys, values, span_mask, section, section_gate):
    rows, wide = queries.shape
    heads, kv_heads = wide // HEAD_SIZE, keys.shape[1] // HEAD_SIZE
    width = heads // kv_heads * rows
    count = lax.axis_size("tm")
    per_span = CH // rows
    spans = count // per_span
    params = pltpu.CompilerParams(vmem_limit_bytes=24 * 1024 * 1024)
    acc_shape = jax.ShapeDtypeStruct((kv_heads, width, 2 * HEAD_SIZE), jnp.float32)

    def cost(blocks, times=2):
        return pl.CostEstimate(
            flops=4 * times * blocks * rows * rows * wide, bytes_accessed=rows * wide * 8, transcendentals=blocks * rows * rows * heads
        )

    cores = lax.axis_size("head")

    def send(value, target):
        pairs = []
        for i in range(count):
            for core in range(cores):
                if target(i) is None:
                    goal = i * cores + (core + 1) % cores if cores > 1 else i
                else:
                    goal = target(i) * cores + core
                pairs.append((i * cores + core, goal))
        return lax.ppermute(value, ("tm", "head"), pairs)

    def onward(value, distance):
        first = (distance - 1) * per_span

        def target(i):
            if i < first:
                return None
            return i + per_span if i + per_span < count else first + i % per_span

        return send(value, target)

    def around(value, distance, turn):
        return send(
            value, lambda i: i - i % per_span + (i + turn) % per_span if i >= (distance - 1) * per_span else None
        )

    def travel(held, distance, turned_before):
        onwards = [onward(x, distance + 1) for x in held] if distance + 1 < spans else []
        turned = [[around(x, distance, turn) for turn in range(1, per_span)] for x in held]
        if not onwards and turned_before:
            turned[1] = [onward(v, distance) for _, v in turned_before]
        return list(zip(*turned)), onwards

    floor = pl.pallas_call(
        floor_kernel,
        out_shape=jax.ShapeDtypeStruct((8, width), jnp.float32),
        out_specs=VMEM,
        compiler_params=params,
        cost_estimate=cost(4, 10),
        name="floor",
    )()
    held = [onward(x, 1) for x in (keys, values)] if spans > 1 else []
    near_keys, near_values, floor = lax.optimization_barrier((keys, values, floor))
    turned = list(zip(*[[around(x, 0, turn) for turn in range(1, per_span)] for x in (near_keys, near_values)]))
    def prepare(*refs):
        prepare_kernel(per_span, *refs)

    stacked, tails, gate_row, tops = pl.pallas_call(
        prepare,
        out_shape=(
            jax.ShapeDtypeStruct((kv_heads, width, 2 * HEAD_SIZE), jnp.bfloat16),
            jax.ShapeDtypeStruct((spans, rows, HEAD_SIZE), jnp.bfloat16),
            jax.ShapeDtypeStruct((1, wide), jnp.float32),
            jax.ShapeDtypeStruct((heads, rows), jnp.float32),
        ),
        in_specs=[pl.BlockSpec(memory_space=pltpu.SMEM)] * 2 + [VMEM] * 2 + [HBM] * 2,
        out_specs=(VMEM,) * 4,
        scratch_shapes=[
            pltpu.VMEM(queries.shape, queries.dtype),
            pltpu.VMEM(keys.shape, keys.dtype),
            pltpu.SemaphoreType.DMA((2,)),
        ],
        compiler_params=params,
        cost_estimate=cost(1, 10),
        name="prepare",
    )(span_mask, section, section_gate, floor, queries, keys)

    token = tops
    seen_blocks = []
    for distance in range(1, spans):
        waiting = ([(0, (keys, values))] if distance == 1 else []) + [(distance - 1, t) for t in turned]
        forward = []
        for x in held:
            x, token = lax.optimization_barrier((x, token))
            forward.append(x)
        held = forward
        waiting.append((distance, tuple(held)))
        turned, held = travel(held, distance, turned)
        distances = [d for d, _ in waiting]
        blocks = [k for _, (k, _) in waiting] + [v for _, (_, v) in waiting]
        seen_blocks += waiting
        if distance == 1:
            tops, state = token, []
        else:
            state = [token]

        def step(*refs, distances=distances):
            step_kernel(distances, distances[0] == 0, *refs)

        acc = pl.pallas_call(
            step,
            out_shape=acc_shape,
            in_specs=[VMEM] * (2 + len(state) + len(blocks)),
            out_specs=VMEM,
            compiler_params=params,
            cost_estimate=cost(len(waiting)),
            name="step_%d" % distance,
        )(stacked, tails, *state, *blocks)
        token = acc

    distances = [d for d, _ in seen_blocks] + [spans - 1] * len(turned)

    def close(*refs):
        close_kernel(distances, len(turned), *refs)

    blocks = [k for _, (k, _) in seen_blocks] + [k for k, _ in turned] + [v for _, (_, v) in seen_blocks]
    part, last_weight, log_total = pl.pallas_call(
        close,
        out_shape=(
            jax.ShapeDtypeStruct((kv_heads, width, HEAD_SIZE), jnp.float32),
            jax.ShapeDtypeStruct((kv_heads, width, len(turned) * rows), jnp.bfloat16),
            jax.ShapeDtypeStruct((heads, rows), jnp.float32),
        ),
        in_specs=[VMEM] * (5 + len(blocks)),
        out_specs=(VMEM,) * 3,
        compiler_params=params,
        cost_estimate=cost(1),
        name="close",
    )(stacked, tails, gate_row, tops, acc, *blocks)
    mixed = pl.pallas_call(
        mix_kernel,
        out_shape=jax.ShapeDtypeStruct((rows, wide), jnp.bfloat16),
        in_specs=[VMEM] * (3 + len(turned)),
        out_specs=HBM,
        scratch_shapes=[pltpu.VMEM((rows, wide), jnp.bfloat16), pltpu.SemaphoreType.DMA((kv_heads,))],
        compiler_params=params,
        cost_estimate=cost(1),
        name="mix",
    )(gate_row, part, last_weight, *[v for _, v in turned])
    return mixed, log_total


def solution(mesh):
    placed = (
        P(("grp", "tm"), "head"),
        P(("grp", "tm"), "head"),
        P(("grp", "tm"), "head"),
        P("grp", None),
        P("grp"),
        P(None, "head"),
    )
    return jax.shard_map(
        on_device,
        mesh=mesh,
        in_specs=placed,
        out_specs=(P(("grp", "tm"), "head"), P("head", ("grp", "tm"))),
        check_vma=False,
    )
```

```python
import math

import jax
import jax.numpy as jnp
from jax import lax
from jax.experimental import pallas as pl
from jax.experimental.pallas import tpu as pltpu
from jax.sharding import PartitionSpec as P

HEAD_SIZE = 128
CH = 256
LOG2E = math.log2(math.e)
FAR = 1e30
LIMIT = 2.0**80
SCALE = LOG2E / math.sqrt(HEAD_SIZE)
HBM = pl.BlockSpec(memory_space=pltpu.HBM)
VMEM = pl.BlockSpec(memory_space=pltpu.VMEM)


def head_columns(h):
    return slice(h * HEAD_SIZE, (h + 1) * HEAD_SIZE)


def against(queries, keys):
    return lax.dot_general(queries, keys, (((1,), (1,)), ((), ())), preferred_element_type=jnp.float32)


def with_ones(values):
    return jnp.concatenate([values, jnp.ones((values.shape[0], HEAD_SIZE), values.dtype)], axis=1)


def lanes(rows):
    return lax.broadcasted_iota(jnp.int32, (rows, HEAD_SIZE), 1)


def floor_kernel(floor):
    floor[...] = jnp.full(floor.shape, -FAR, jnp.float32)


def own_kernel(per_span, mask, section, gate, floor, q_hbm, k_hbm, v_hbm,
               stacked, tails, gate_row, tops, acc, q, k, v, sems):
    copies = [
        pltpu.make_async_copy(src, dst, sems.at[i])
        for i, (src, dst) in enumerate([(q_hbm, q), (k_hbm, k), (v_hbm, v)])
    ]
    for copy in copies:
        copy.start()
    span = lax.axis_index("tm") // per_span
    at = lanes(tails.shape[1])
    for distance in range(tails.shape[0]):
        allowed = jnp.logical_and(span >= distance, mask[span, jnp.maximum(span - distance, 0)] > 0)
        bias = jnp.where(allowed, 0.0, -FAR)
        tails[distance] = jnp.where(at < 3, 1.0, jnp.where(at == 3, bias, 0.0)).astype(jnp.bfloat16)
    gate_row[...] = gate[pl.ds(section[span], 1), :]
    for copy in copies:
        copy.wait()
    rows, width = q.shape[0], stacked.shape[1]
    group = width // rows
    at = lanes(1)
    for h in range(stacked.shape[0]):
        queries = jnp.concatenate([q[:, head_columns(h * group + g)] for g in range(group)], axis=0)
        score = against(queries, k[:, head_columns(h)])
        top = jnp.maximum(floor[0:1, 0:1], jnp.max(jnp.max(score, axis=0, keepdims=True), axis=1, keepdims=True))
        weight = jnp.exp2(SCALE * (score - top)).astype(jnp.bfloat16)
        acc[h] = jnp.dot(weight, with_ones(v[:, head_columns(h)]), preferred_element_type=jnp.float32)
        high = top.astype(jnp.bfloat16).astype(jnp.float32)
        middle = (top - high).astype(jnp.bfloat16).astype(jnp.float32)
        low = top - high - middle
        extra = jnp.where(at == 0, -high, jnp.where(at == 1, -middle, jnp.where(at == 2, -low, jnp.where(at == 3, 1.0, 0.0))))
        extra = jnp.broadcast_to(extra, (width, HEAD_SIZE)).astype(jnp.bfloat16)
        stacked[h] = jnp.concatenate([queries, extra], axis=1)
        tops[h * group : (h + 1) * group, :] = jnp.broadcast_to(top * (1.0 / math.sqrt(HEAD_SIZE)), (group, rows))


def weights_of(h, distances, stacked, tails, key_refs):
    keys = jnp.concatenate(
        [jnp.concatenate([k[:, head_columns(h)], tails[d]], axis=1) for d, k in zip(distances, key_refs)], axis=0
    )
    return jnp.exp2(SCALE * against(stacked[h], keys))


def step_kernel(distances, stacked, tails, acc_in, *refs):
    count = len(distances)
    key_refs, value_refs, (acc,) = refs[:count], refs[count : 2 * count], refs[2 * count :]
    for h in range(stacked.shape[0]):
        weight = weights_of(h, distances, stacked, tails, key_refs).astype(jnp.bfloat16)
        values = with_ones(jnp.concatenate([v[:, head_columns(h)] for v in value_refs], axis=0))
        acc[h] = acc_in[h] + jnp.dot(weight, values, preferred_element_type=jnp.float32)


def close_kernel(distances, last, stacked, tails, gate_row, tops, acc, *refs):
    count = len(distances)
    key_refs, value_refs, (part, last_weight, log_ref) = refs[:count], refs[count : 2 * count - last], refs[2 * count - last :]
    heads, rows = log_ref.shape
    width = stacked.shape[1]
    group = width // rows
    at = lanes(rows)

    def gated(h, g, attended):
        columns = pl.ds(pl.multiple_of((h * group + g) * HEAD_SIZE, HEAD_SIZE), HEAD_SIZE)
        part[h, g * rows : (g + 1) * rows, :] = attended[g * rows : (g + 1) * rows, :] * gate_row[:, columns]

    every_total = jnp.ones((rows, HEAD_SIZE), jnp.float32)
    for h in range(stacked.shape[0]):
        weight = weights_of(h, distances[-last:], stacked, tails, key_refs[-last:])
        ones = jnp.ones((weight.shape[1], HEAD_SIZE), jnp.bfloat16)
        total = acc[h, :, HEAD_SIZE:] + jnp.dot(weight.astype(jnp.bfloat16), ones, preferred_element_type=jnp.float32)
        inverse = pl.reciprocal(total, approx=True)
        inverse = inverse * (2.0 - total * inverse)
        for i in range(last):
            last_weight[h, :, head_columns(i)] = (weight[:, head_columns(i)] * inverse).astype(jnp.bfloat16)
        attended = acc[h, :, :HEAD_SIZE] * inverse
        for g in range(group):
            gated(h, g, attended)
            every_total = jnp.where(at == h * group + g, total[g * rows : (g + 1) * rows, :], every_total)
    log_ref[...] = tops[...] + jnp.log(every_total.T[:heads, :])
    fits = jnp.logical_and(every_total <= LIMIT, every_total >= 1.0 / LIMIT)
    outside = jnp.max(jnp.where(fits, 0.0, 1.0))

    @pl.when(outside > 0.0)
    def _():
        def one_head(h, carry):
            every_top, every_total = carry
            inside = pl.ds(pl.multiple_of(h * HEAD_SIZE, HEAD_SIZE), HEAD_SIZE)
            queries = stacked[h, :, :HEAD_SIZE]
            bias = [tails[d, 0:1, 3:4].astype(jnp.float32) for d in distances]
            top = None
            for k, b in zip(key_refs, bias):
                row = jnp.max(against(queries, k[:, inside]) + b, axis=1, keepdims=True)
                top = row if top is None else jnp.maximum(top, row)
            total = jnp.zeros((width, 1), jnp.float32)
            attended = jnp.zeros((width, HEAD_SIZE), jnp.float32)
            late = []
            for i, (k, b) in enumerate(zip(key_refs, bias)):
                weight = jnp.exp2(SCALE * (against(queries, k[:, inside]) + b - top))
                total += jnp.sum(weight, axis=1, keepdims=True)
                if i < count - last:
                    attended += jnp.dot(
                        weight.astype(jnp.bfloat16), value_refs[i][:, inside], preferred_element_type=jnp.float32
                    )
                else:
                    late.append(weight)
            inverse = 1.0 / total
            for i, weight in enumerate(late):
                last_weight[h, :, head_columns(i)] = (weight * inverse).astype(jnp.bfloat16)
            attended = attended * inverse
            for g in range(group):
                gated(h, g, attended)
                here = at == h * group + g
                every_top = jnp.where(here, top[g * rows : (g + 1) * rows, :], every_top)
                every_total = jnp.where(here, total[g * rows : (g + 1) * rows, :], every_total)
            return every_top, every_total

        start = (jnp.zeros((rows, HEAD_SIZE), jnp.float32), jnp.ones((rows, HEAD_SIZE), jnp.float32))
        every_top, every_total = lax.fori_loop(0, stacked.shape[0], one_head, start)
        log_ref[...] = (every_top.T * (1.0 / math.sqrt(HEAD_SIZE)) + jnp.log(every_total.T))[:heads, :]


def mix_kernel(gate_row, part, last_weight, *refs):
    value_refs, (mixed_hbm, mixed, sems) = refs[:-3], refs[-3:]
    kv_heads, width = part.shape[0], part.shape[1]
    rows = mixed.shape[0]
    group = width // rows
    copies = []
    for h in range(kv_heads):
        values = jnp.concatenate([v[:, head_columns(h)] for v in value_refs], axis=0)
        rest = jnp.dot(last_weight[h], values, preferred_element_type=jnp.float32)
        for g in range(group):
            inside = slice(g * rows, (g + 1) * rows)
            columns = head_columns(h * group + g)
            mixed[:, columns] = (part[h, inside, :] + gate_row[:, columns] * rest[inside, :]).astype(jnp.bfloat16)
        columns = pl.ds(h * group * HEAD_SIZE, group * HEAD_SIZE)
        copies.append(pltpu.make_async_copy(mixed.at[:, columns], mixed_hbm.at[:, columns], sems.at[h]))
        copies[-1].start()
    for copy in copies:
        copy.wait()


def on_device(queries, keys, values, span_mask, section, section_gate):
    rows, wide = queries.shape
    heads, kv_heads = wide // HEAD_SIZE, keys.shape[1] // HEAD_SIZE
    width = heads // kv_heads * rows
    count = lax.axis_size("tm")
    per_span = CH // rows
    spans = count // per_span
    params = pltpu.CompilerParams(vmem_limit_bytes=24 * 1024 * 1024)
    acc_shape = jax.ShapeDtypeStruct((kv_heads, width, 2 * HEAD_SIZE), jnp.float32)

    def cost(blocks, times=3):
        return pl.CostEstimate(
            flops=4 * times * blocks * rows * rows * wide, bytes_accessed=rows * wide * 8, transcendentals=blocks * rows * rows * heads
        )

    cores = lax.axis_size("head")

    def send(value, target):
        pairs = []
        for i in range(count):
            for core in range(cores):
                if target(i) is None:
                    goal = i * cores + (core + 1) % cores if cores > 1 else i
                else:
                    goal = target(i) * cores + core
                pairs.append((i * cores + core, goal))
        return lax.ppermute(value, ("tm", "head"), pairs)

    def onward(value, distance):
        first = (distance - 1) * per_span

        def target(i):
            if i < first:
                return None
            return i + per_span if i + per_span < count else first + i % per_span

        return send(value, target)

    def around(value, distance, turn):
        return send(
            value, lambda i: i - i % per_span + (i + turn) % per_span if i >= distance * per_span else None
        )

    def travel(held, distance, turned_before):
        onwards = [onward(x, distance + 1) for x in held] if distance + 1 < spans else []
        turned = [[around(x, distance, turn) for turn in range(1, per_span)] for x in held]
        if not onwards and turned_before:
            turned[1] = [onward(v, distance) for _, v in turned_before]
        return list(zip(*turned)), onwards

    floor = pl.pallas_call(
        floor_kernel,
        out_shape=jax.ShapeDtypeStruct((8, width), jnp.float32),
        out_specs=VMEM,
        compiler_params=params,
        cost_estimate=cost(4, 10),
        name="floor",
    )()
    held = [onward(x, 1) for x in (keys, values)] if spans > 1 else []
    near_keys, near_values, floor = lax.optimization_barrier((keys, values, floor))
    turned = list(zip(*[[around(x, 0, turn) for turn in range(1, per_span)] for x in (near_keys, near_values)]))
    def own(*refs):
        own_kernel(per_span, *refs)

    stacked, tails, gate_row, tops, acc = pl.pallas_call(
        own,
        out_shape=(
            jax.ShapeDtypeStruct((kv_heads, width, 2 * HEAD_SIZE), jnp.bfloat16),
            jax.ShapeDtypeStruct((spans, rows, HEAD_SIZE), jnp.bfloat16),
            jax.ShapeDtypeStruct((1, wide), jnp.float32),
            jax.ShapeDtypeStruct((heads, rows), jnp.float32),
            acc_shape,
        ),
        in_specs=[pl.BlockSpec(memory_space=pltpu.SMEM)] * 2 + [VMEM] * 2 + [HBM] * 3,
        out_specs=(VMEM,) * 5,
        scratch_shapes=[
            pltpu.VMEM(queries.shape, queries.dtype),
            pltpu.VMEM(keys.shape, keys.dtype),
            pltpu.VMEM(values.shape, values.dtype),
            pltpu.SemaphoreType.DMA((3,)),
        ],
        compiler_params=params,
        cost_estimate=cost(1, 5),
        name="own",
    )(span_mask, section, section_gate, floor, queries, keys, values)

    seen_blocks = [(0, (keys, values))]
    for distance in range(1, spans):
        waiting = [(distance - 1, t) for t in turned]
        forward = []
        for x in held:
            x, acc = lax.optimization_barrier((x, acc))
            forward.append(x)
        held = forward
        waiting.append((distance, tuple(held)))
        turned, held = travel(held, distance, turned)
        distances = [d for d, _ in waiting]
        blocks = [k for _, (k, _) in waiting] + [v for _, (_, v) in waiting]
        seen_blocks += waiting

        def step(*refs, distances=distances):
            step_kernel(distances, *refs)

        acc = pl.pallas_call(
            step,
            out_shape=acc_shape,
            in_specs=[VMEM] * (3 + len(blocks)),
            out_specs=VMEM,
            compiler_params=params,
            cost_estimate=cost(len(waiting)),
            name="step_%d" % distance,
        )(stacked, tails, acc, *blocks)

    distances = [d for d, _ in seen_blocks] + [spans - 1] * len(turned)

    def close(*refs):
        close_kernel(distances, len(turned), *refs)

    blocks = [k for _, (k, _) in seen_blocks] + [k for k, _ in turned] + [v for _, (_, v) in seen_blocks]
    part, last_weight, log_total = pl.pallas_call(
        close,
        out_shape=(
            jax.ShapeDtypeStruct((kv_heads, width, HEAD_SIZE), jnp.float32),
            jax.ShapeDtypeStruct((kv_heads, width, len(turned) * rows), jnp.bfloat16),
            jax.ShapeDtypeStruct((heads, rows), jnp.float32),
        ),
        in_specs=[VMEM] * (5 + len(blocks)),
        out_specs=(VMEM,) * 3,
        compiler_params=params,
        cost_estimate=cost(2),
        name="close",
    )(stacked, tails, gate_row, tops, acc, *blocks)
    mixed = pl.pallas_call(
        mix_kernel,
        out_shape=jax.ShapeDtypeStruct((rows, wide), jnp.bfloat16),
        in_specs=[VMEM] * (3 + len(turned)),
        out_specs=HBM,
        scratch_shapes=[pltpu.VMEM((rows, wide), jnp.bfloat16), pltpu.SemaphoreType.DMA((kv_heads,))],
        compiler_params=params,
        cost_estimate=cost(2),
        name="mix",
    )(gate_row, part, last_weight, *[v for _, v in turned])
    return mixed, log_total


def solution(mesh):
    placed = (
        P(("grp", "tm"), "head"),
        P(("grp", "tm"), "head"),
        P(("grp", "tm"), "head"),
        P("grp", None),
        P("grp"),
        P(None, "head"),
    )
    return jax.shard_map(
        on_device,
        mesh=mesh,
        in_specs=placed,
        out_specs=(P(("grp", "tm"), "head"), P("head", ("grp", "tm"))),
        check_vma=False,
    )
```

```python
import math

import jax
import jax.numpy as jnp
from jax import lax
from jax.experimental import pallas as pl
from jax.experimental.pallas import tpu as pltpu
from jax.sharding import PartitionSpec as P

HEAD_SIZE = 128
CH = 256
LOG2E = math.log2(math.e)
FAR = 1e30
LIMIT = 2.0**80
SCALE = LOG2E / math.sqrt(HEAD_SIZE)
HBM = pl.BlockSpec(memory_space=pltpu.HBM)
VMEM = pl.BlockSpec(memory_space=pltpu.VMEM)


def head_columns(h):
    return slice(h * HEAD_SIZE, (h + 1) * HEAD_SIZE)


def against(queries, keys):
    return lax.dot_general(queries, keys, (((1,), (1,)), ((), ())), preferred_element_type=jnp.float32)


def with_ones(values):
    return jnp.concatenate([values, jnp.ones((values.shape[0], HEAD_SIZE), values.dtype)], axis=1)


def lanes(rows):
    return lax.broadcasted_iota(jnp.int32, (rows, HEAD_SIZE), 1)


def floor_kernel(floor):
    floor[...] = jnp.full(floor.shape, -FAR, jnp.float32)


def own_kernel(per_span, mask, section, gate, floor, q_hbm, k_hbm, v_hbm,
               stacked, tails, gate_row, tops, acc, q, k, v, sems):
    copies = [
        pltpu.make_async_copy(src, dst, sems.at[i])
        for i, (src, dst) in enumerate([(q_hbm, q), (k_hbm, k), (v_hbm, v)])
    ]
    for copy in copies:
        copy.start()
    span = lax.axis_index("tm") // per_span
    at = lanes(tails.shape[1])
    for distance in range(tails.shape[0]):
        allowed = jnp.logical_and(span >= distance, mask[span, jnp.maximum(span - distance, 0)] > 0)
        bias = jnp.where(allowed, 0.0, -FAR)
        tails[distance] = jnp.where(at < 3, 1.0, jnp.where(at == 3, bias, 0.0)).astype(jnp.bfloat16)
    gate_row[...] = gate[pl.ds(section[span], 1), :]
    for copy in copies:
        copy.wait()
    rows, width = q.shape[0], stacked.shape[1]
    group = width // rows
    at = lanes(1)
    for h in range(stacked.shape[0]):
        queries = jnp.concatenate([q[:, head_columns(h * group + g)] for g in range(group)], axis=0)
        score = against(queries, k[:, head_columns(h)])
        top = jnp.maximum(floor[0:1, 0:1], jnp.max(jnp.max(score, axis=0, keepdims=True), axis=1, keepdims=True))
        weight = jnp.exp2(SCALE * (score - top)).astype(jnp.bfloat16)
        acc[h] = jnp.dot(weight, with_ones(v[:, head_columns(h)]), preferred_element_type=jnp.float32)
        high = top.astype(jnp.bfloat16).astype(jnp.float32)
        middle = (top - high).astype(jnp.bfloat16).astype(jnp.float32)
        low = top - high - middle
        extra = jnp.where(at == 0, -high, jnp.where(at == 1, -middle, jnp.where(at == 2, -low, jnp.where(at == 3, 1.0, 0.0))))
        extra = jnp.broadcast_to(extra, (width, HEAD_SIZE)).astype(jnp.bfloat16)
        stacked[h] = jnp.concatenate([queries, extra], axis=1)
        tops[h * group : (h + 1) * group, :] = jnp.broadcast_to(top * (1.0 / math.sqrt(HEAD_SIZE)), (group, rows))


def weights_of(h, distances, stacked, tails, key_refs):
    keys = jnp.concatenate(
        [jnp.concatenate([k[:, head_columns(h)], tails[d]], axis=1) for d, k in zip(distances, key_refs)], axis=0
    )
    return jnp.exp2(SCALE * against(stacked[h], keys))


def step_kernel(distances, stacked, tails, acc_in, *refs):
    count = len(distances)
    key_refs, value_refs, (acc,) = refs[:count], refs[count : 2 * count], refs[2 * count :]
    for h in range(stacked.shape[0]):
        weight = weights_of(h, distances, stacked, tails, key_refs).astype(jnp.bfloat16)
        values = with_ones(jnp.concatenate([v[:, head_columns(h)] for v in value_refs], axis=0))
        acc[h] = acc_in[h] + jnp.dot(weight, values, preferred_element_type=jnp.float32)


def close_kernel(distances, last, stacked, tails, gate_row, tops, acc, *refs):
    count = len(distances)
    key_refs, value_refs, (part, last_weight, log_ref) = refs[:count], refs[count : 2 * count - last], refs[2 * count - last :]
    heads, rows = log_ref.shape
    width = stacked.shape[1]
    group = width // rows
    at = lanes(rows)

    def gated(h, g, attended):
        columns = pl.ds(pl.multiple_of((h * group + g) * HEAD_SIZE, HEAD_SIZE), HEAD_SIZE)
        part[h, g * rows : (g + 1) * rows, :] = attended[g * rows : (g + 1) * rows, :] * gate_row[:, columns]

    every_total = jnp.ones((rows, HEAD_SIZE), jnp.float32)
    for h in range(stacked.shape[0]):
        weight = weights_of(h, distances[-last:], stacked, tails, key_refs[-last:])
        ones = jnp.ones((weight.shape[1], HEAD_SIZE), jnp.bfloat16)
        total = acc[h, :, HEAD_SIZE:] + jnp.dot(weight.astype(jnp.bfloat16), ones, preferred_element_type=jnp.float32)
        inverse = pl.reciprocal(total, approx=True)
        inverse = inverse * (2.0 - total * inverse)
        for i in range(last):
            last_weight[h, :, head_columns(i)] = (weight[:, head_columns(i)] * inverse).astype(jnp.bfloat16)
        attended = acc[h, :, :HEAD_SIZE] * inverse
        for g in range(group):
            gated(h, g, attended)
            every_total = jnp.where(at == h * group + g, total[g * rows : (g + 1) * rows, :], every_total)
    log_ref[...] = tops[...] + jnp.log(every_total.T[:heads, :])
    fits = jnp.logical_and(every_total <= LIMIT, every_total >= 1.0 / LIMIT)
    outside = jnp.max(jnp.where(fits, 0.0, 1.0))

    @pl.when(outside > 0.0)
    def _():
        def one_head(h, carry):
            every_top, every_total = carry
            inside = pl.ds(pl.multiple_of(h * HEAD_SIZE, HEAD_SIZE), HEAD_SIZE)
            queries = stacked[h, :, :HEAD_SIZE]
            bias = [tails[d, 0:1, 3:4].astype(jnp.float32) for d in distances]
            top = None
            for k, b in zip(key_refs, bias):
                row = jnp.max(against(queries, k[:, inside]) + b, axis=1, keepdims=True)
                top = row if top is None else jnp.maximum(top, row)
            total = jnp.zeros((width, 1), jnp.float32)
            attended = jnp.zeros((width, HEAD_SIZE), jnp.float32)
            late = []
            for i, (k, b) in enumerate(zip(key_refs, bias)):
                weight = jnp.exp2(SCALE * (against(queries, k[:, inside]) + b - top))
                total += jnp.sum(weight, axis=1, keepdims=True)
                if i < count - last:
                    attended += jnp.dot(
                        weight.astype(jnp.bfloat16), value_refs[i][:, inside], preferred_element_type=jnp.float32
                    )
                else:
                    late.append(weight)
            inverse = 1.0 / total
            for i, weight in enumerate(late):
                last_weight[h, :, head_columns(i)] = (weight * inverse).astype(jnp.bfloat16)
            attended = attended * inverse
            for g in range(group):
                gated(h, g, attended)
                here = at == h * group + g
                every_top = jnp.where(here, top[g * rows : (g + 1) * rows, :], every_top)
                every_total = jnp.where(here, total[g * rows : (g + 1) * rows, :], every_total)
            return every_top, every_total

        start = (jnp.zeros((rows, HEAD_SIZE), jnp.float32), jnp.ones((rows, HEAD_SIZE), jnp.float32))
        every_top, every_total = lax.fori_loop(0, stacked.shape[0], one_head, start)
        log_ref[...] = (every_top.T * (1.0 / math.sqrt(HEAD_SIZE)) + jnp.log(every_total.T))[:heads, :]


def mix_kernel(gate_row, part, last_weight, *refs):
    value_refs, (mixed_hbm, mixed, sems) = refs[:-3], refs[-3:]
    kv_heads, width = part.shape[0], part.shape[1]
    rows = mixed.shape[0]
    group = width // rows
    copies = []
    for h in range(kv_heads):
        values = jnp.concatenate([v[:, head_columns(h)] for v in value_refs], axis=0)
        rest = jnp.dot(last_weight[h], values, preferred_element_type=jnp.float32)
        for g in range(group):
            inside = slice(g * rows, (g + 1) * rows)
            columns = head_columns(h * group + g)
            mixed[:, columns] = (part[h, inside, :] + gate_row[:, columns] * rest[inside, :]).astype(jnp.bfloat16)
        columns = pl.ds(h * group * HEAD_SIZE, group * HEAD_SIZE)
        copies.append(pltpu.make_async_copy(mixed.at[:, columns], mixed_hbm.at[:, columns], sems.at[h]))
        copies[-1].start()
    for copy in copies:
        copy.wait()


def on_device(queries, keys, values, span_mask, section, section_gate):
    rows, wide = queries.shape
    heads, kv_heads = wide // HEAD_SIZE, keys.shape[1] // HEAD_SIZE
    width = heads // kv_heads * rows
    count = lax.axis_size("tm")
    per_span = CH // rows
    spans = count // per_span
    params = pltpu.CompilerParams(vmem_limit_bytes=24 * 1024 * 1024)
    acc_shape = jax.ShapeDtypeStruct((kv_heads, width, 2 * HEAD_SIZE), jnp.float32)

    def cost(blocks, times=3):
        return pl.CostEstimate(
            flops=4 * times * blocks * rows * rows * wide, bytes_accessed=rows * wide * 8, transcendentals=blocks * rows * rows * heads
        )

    cores = lax.axis_size("head")

    def send(value, target):
        pairs = []
        for i in range(count):
            for core in range(cores):
                if target(i) is None:
                    goal = i * cores + (core + 1) % cores if cores > 1 else i
                else:
                    goal = target(i) * cores + core
                pairs.append((i * cores + core, goal))
        return lax.ppermute(value, ("tm", "head"), pairs)

    def onward(value, distance):
        first = (distance - 1) * per_span

        def target(i):
            if i < first:
                return None
            return i + per_span if i + per_span < count else first + i % per_span

        return send(value, target)

    def around(value, distance, turn):
        return send(
            value, lambda i: i - i % per_span + (i + turn) % per_span if i >= distance * per_span else None
        )

    def leap(value):
        return send(value, lambda i: (i - per_span) % count)

    def travel(held, distance, far_values):
        onwards = [onward(x, distance + 1) for x in held] if distance + 1 < spans else []
        turned = [[around(x, distance, turn) for turn in range(1, per_span)] for x in (held if onwards else held[:1])]
        if not onwards:
            turned.append(far_values)
        return list(zip(*turned)), onwards

    floor = pl.pallas_call(
        floor_kernel,
        out_shape=jax.ShapeDtypeStruct((8, width), jnp.float32),
        out_specs=VMEM,
        compiler_params=params,
        cost_estimate=cost(4, 10),
        name="floor",
    )()
    held = [onward(x, 1) for x in (keys, values)] if spans > 1 else []
    near_keys, near_values, floor = lax.optimization_barrier((keys, values, floor))
    turned = list(zip(*[[around(x, 0, turn) for turn in range(1, per_span)] for x in (near_keys, near_values)]))
    def own(*refs):
        own_kernel(per_span, *refs)

    stacked, tails, gate_row, tops, acc = pl.pallas_call(
        own,
        out_shape=(
            jax.ShapeDtypeStruct((kv_heads, width, 2 * HEAD_SIZE), jnp.bfloat16),
            jax.ShapeDtypeStruct((spans, rows, HEAD_SIZE), jnp.bfloat16),
            jax.ShapeDtypeStruct((1, wide), jnp.float32),
            jax.ShapeDtypeStruct((heads, rows), jnp.float32),
            acc_shape,
        ),
        in_specs=[pl.BlockSpec(memory_space=pltpu.SMEM)] * 2 + [VMEM] * 2 + [HBM] * 3,
        out_specs=(VMEM,) * 5,
        scratch_shapes=[
            pltpu.VMEM(queries.shape, queries.dtype),
            pltpu.VMEM(keys.shape, keys.dtype),
            pltpu.VMEM(values.shape, values.dtype),
            pltpu.SemaphoreType.DMA((3,)),
        ],
        compiler_params=params,
        cost_estimate=cost(1, 5),
        name="own",
    )(span_mask, section, section_gate, floor, queries, keys, values)

    beside = [v for _, v in turned]
    far_values = [leap(v) for v in beside] if spans == 2 else None
    seen_blocks = [(0, (keys, values))]
    for distance in range(1, spans):
        waiting = [(distance - 1, t) for t in turned]
        forward = []
        for x in held:
            x, acc = lax.optimization_barrier((x, acc))
            forward.append(x)
        held = forward
        waiting.append((distance, tuple(held)))
        turned, held = travel(held, distance, far_values)
        distances = [d for d, _ in waiting]
        blocks = [k for _, (k, _) in waiting] + [v for _, (_, v) in waiting]
        seen_blocks += waiting

        def step(*refs, distances=distances):
            step_kernel(distances, *refs)

        acc = pl.pallas_call(
            step,
            out_shape=acc_shape,
            in_specs=[VMEM] * (3 + len(blocks)),
            out_specs=VMEM,
            compiler_params=params,
            cost_estimate=cost(len(waiting)),
            name="step_%d" % distance,
        )(stacked, tails, acc, *blocks)
        if far_values is None:
            far_values = []
            for x in beside:
                x, acc = lax.optimization_barrier((x, acc))
                far_values.append(leap(x))

    distances = [d for d, _ in seen_blocks] + [spans - 1] * len(turned)

    def close(*refs):
        close_kernel(distances, len(turned), *refs)

    blocks = [k for _, (k, _) in seen_blocks] + [k for k, _ in turned] + [v for _, (_, v) in seen_blocks]
    part, last_weight, log_total = pl.pallas_call(
        close,
        out_shape=(
            jax.ShapeDtypeStruct((kv_heads, width, HEAD_SIZE), jnp.float32),
            jax.ShapeDtypeStruct((kv_heads, width, len(turned) * rows), jnp.bfloat16),
            jax.ShapeDtypeStruct((heads, rows), jnp.float32),
        ),
        in_specs=[VMEM] * (5 + len(blocks)),
        out_specs=(VMEM,) * 3,
        compiler_params=params,
        cost_estimate=cost(2),
        name="close",
    )(stacked, tails, gate_row, tops, acc, *blocks)
    mixed = pl.pallas_call(
        mix_kernel,
        out_shape=jax.ShapeDtypeStruct((rows, wide), jnp.bfloat16),
        in_specs=[VMEM] * (3 + len(turned)),
        out_specs=HBM,
        scratch_shapes=[pltpu.VMEM((rows, wide), jnp.bfloat16), pltpu.SemaphoreType.DMA((kv_heads,))],
        compiler_params=params,
        cost_estimate=cost(2),
        name="mix",
    )(gate_row, part, last_weight, *[v for _, v in turned])
    return mixed, log_total


def solution(mesh):
    placed = (
        P(("grp", "tm"), "head"),
        P(("grp", "tm"), "head"),
        P(("grp", "tm"), "head"),
        P("grp", None),
        P("grp"),
        P(None, "head"),
    )
    return jax.shard_map(
        on_device,
        mesh=mesh,
        in_specs=placed,
        out_specs=(P(("grp", "tm"), "head"), P("head", ("grp", "tm"))),
        check_vma=False,
    )
```

```python
import math

import jax
import jax.numpy as jnp
from jax import lax
from jax.experimental import pallas as pl
from jax.experimental.pallas import tpu as pltpu
from jax.sharding import PartitionSpec as P

HEAD_SIZE = 128
CH = 256
LOG2E = math.log2(math.e)
FAR = 1e30
LIMIT = 2.0**80
SCALE = LOG2E / math.sqrt(HEAD_SIZE)
HBM = pl.BlockSpec(memory_space=pltpu.HBM)
VMEM = pl.BlockSpec(memory_space=pltpu.VMEM)


def head_columns(h):
    return slice(h * HEAD_SIZE, (h + 1) * HEAD_SIZE)


def against(queries, keys):
    return lax.dot_general(queries, keys, (((1,), (1,)), ((), ())), preferred_element_type=jnp.float32)


def with_ones(values):
    return jnp.concatenate([values, jnp.ones((values.shape[0], HEAD_SIZE), values.dtype)], axis=1)


def lanes(rows):
    return lax.broadcasted_iota(jnp.int32, (rows, HEAD_SIZE), 1)


def floor_kernel(floor):
    floor[...] = jnp.full(floor.shape, -FAR, jnp.float32)


def own_kernel(per_span, mask, section, gate, floor, q_hbm, k_hbm, v_hbm,
               stacked, tails, gate_row, tops, acc, q, k, v, sems):
    copies = [
        pltpu.make_async_copy(src, dst, sems.at[i])
        for i, (src, dst) in enumerate([(q_hbm, q), (k_hbm, k), (v_hbm, v)])
    ]
    for copy in copies:
        copy.start()
    span = lax.axis_index("tm") // per_span
    at = lanes(tails.shape[1])
    for distance in range(tails.shape[0]):
        allowed = jnp.logical_and(span >= distance, mask[span, jnp.maximum(span - distance, 0)] > 0)
        bias = jnp.where(allowed, 0.0, -FAR)
        tails[distance] = jnp.where(at < 3, 1.0, jnp.where(at == 3, bias, 0.0)).astype(jnp.bfloat16)
    gate_row[...] = gate[pl.ds(section[span], 1), :]
    for copy in copies:
        copy.wait()
    rows, width = q.shape[0], stacked.shape[1]
    group = width // rows
    at = lanes(1)
    for h in range(stacked.shape[0]):
        queries = jnp.concatenate([q[:, head_columns(h * group + g)] for g in range(group)], axis=0)
        score = against(queries, k[:, head_columns(h)])
        top = jnp.maximum(floor[0:1, 0:1], jnp.max(jnp.max(score, axis=0, keepdims=True), axis=1, keepdims=True))
        weight = jnp.exp2(SCALE * (score - top)).astype(jnp.bfloat16)
        acc[h] = jnp.dot(weight, with_ones(v[:, head_columns(h)]), preferred_element_type=jnp.float32)
        high = top.astype(jnp.bfloat16).astype(jnp.float32)
        middle = (top - high).astype(jnp.bfloat16).astype(jnp.float32)
        low = top - high - middle
        extra = jnp.where(at == 0, -high, jnp.where(at == 1, -middle, jnp.where(at == 2, -low, jnp.where(at == 3, 1.0, 0.0))))
        extra = jnp.broadcast_to(extra, (width, HEAD_SIZE)).astype(jnp.bfloat16)
        stacked[h] = jnp.concatenate([queries, extra], axis=1)
        tops[h * group : (h + 1) * group, :] = jnp.broadcast_to(top * (1.0 / math.sqrt(HEAD_SIZE)), (group, rows))


def weights_of(h, distances, stacked, tails, key_refs):
    keys = jnp.concatenate(
        [jnp.concatenate([k[:, head_columns(h)], tails[d]], axis=1) for d, k in zip(distances, key_refs)], axis=0
    )
    return jnp.exp2(SCALE * against(stacked[h], keys))


def step_kernel(distances, stacked, tails, acc_in, *refs):
    count = len(distances)
    key_refs, value_refs, (acc,) = refs[:count], refs[count : 2 * count], refs[2 * count :]
    for h in range(stacked.shape[0]):
        weight = weights_of(h, distances, stacked, tails, key_refs).astype(jnp.bfloat16)
        values = with_ones(jnp.concatenate([v[:, head_columns(h)] for v in value_refs], axis=0))
        acc[h] = acc_in[h] + jnp.dot(weight, values, preferred_element_type=jnp.float32)


def close_kernel(distances, last, stacked, tails, gate_row, tops, acc, *refs):
    count = len(distances)
    key_refs, value_refs, (part, last_weight, log_ref) = refs[:count], refs[count : 2 * count - last], refs[2 * count - last :]
    heads, rows = log_ref.shape
    width = stacked.shape[1]
    group = width // rows
    at = lanes(rows)

    def gated(h, g, attended):
        columns = pl.ds(pl.multiple_of((h * group + g) * HEAD_SIZE, HEAD_SIZE), HEAD_SIZE)
        part[h, g * rows : (g + 1) * rows, :] = attended[g * rows : (g + 1) * rows, :] * gate_row[:, columns]

    every_total = jnp.ones((rows, HEAD_SIZE), jnp.float32)
    for h in range(stacked.shape[0]):
        weight = weights_of(h, distances[-last:], stacked, tails, key_refs[-last:])
        ones = jnp.ones((weight.shape[1], HEAD_SIZE), jnp.bfloat16)
        total = acc[h, :, HEAD_SIZE:] + jnp.dot(weight.astype(jnp.bfloat16), ones, preferred_element_type=jnp.float32)
        inverse = pl.reciprocal(total, approx=True)
        inverse = inverse * (2.0 - total * inverse)
        for i in range(last):
            last_weight[h, :, head_columns(i)] = (weight[:, head_columns(i)] * inverse).astype(jnp.bfloat16)
        attended = acc[h, :, :HEAD_SIZE] * inverse
        for g in range(group):
            gated(h, g, attended)
            every_total = jnp.where(at == h * group + g, total[g * rows : (g + 1) * rows, :], every_total)
    log_ref[...] = tops[...] + jnp.log(every_total.T[:heads, :])
    fits = jnp.logical_and(every_total <= LIMIT, every_total >= 1.0 / LIMIT)
    outside = jnp.max(jnp.where(fits, 0.0, 1.0))

    @pl.when(outside > 0.0)
    def _():
        def one_head(h, carry):
            every_top, every_total = carry
            inside = pl.ds(pl.multiple_of(h * HEAD_SIZE, HEAD_SIZE), HEAD_SIZE)
            queries = stacked[h, :, :HEAD_SIZE]
            bias = [tails[d, 0:1, 3:4].astype(jnp.float32) for d in distances]
            top = None
            for k, b in zip(key_refs, bias):
                row = jnp.max(against(queries, k[:, inside]) + b, axis=1, keepdims=True)
                top = row if top is None else jnp.maximum(top, row)
            total = jnp.zeros((width, 1), jnp.float32)
            attended = jnp.zeros((width, HEAD_SIZE), jnp.float32)
            late = []
            for i, (k, b) in enumerate(zip(key_refs, bias)):
                weight = jnp.exp2(SCALE * (against(queries, k[:, inside]) + b - top))
                total += jnp.sum(weight, axis=1, keepdims=True)
                if i < count - last:
                    attended += jnp.dot(
                        weight.astype(jnp.bfloat16), value_refs[i][:, inside], preferred_element_type=jnp.float32
                    )
                else:
                    late.append(weight)
            inverse = 1.0 / total
            for i, weight in enumerate(late):
                last_weight[h, :, head_columns(i)] = (weight * inverse).astype(jnp.bfloat16)
            attended = attended * inverse
            for g in range(group):
                gated(h, g, attended)
                here = at == h * group + g
                every_top = jnp.where(here, top[g * rows : (g + 1) * rows, :], every_top)
                every_total = jnp.where(here, total[g * rows : (g + 1) * rows, :], every_total)
            return every_top, every_total

        start = (jnp.zeros((rows, HEAD_SIZE), jnp.float32), jnp.ones((rows, HEAD_SIZE), jnp.float32))
        every_top, every_total = lax.fori_loop(0, stacked.shape[0], one_head, start)
        log_ref[...] = (every_top.T * (1.0 / math.sqrt(HEAD_SIZE)) + jnp.log(every_total.T))[:heads, :]


def mix_kernel(gate_row, part, last_weight, *refs):
    value_refs, (mixed_hbm, mixed, sems) = refs[:-3], refs[-3:]
    kv_heads, width = part.shape[0], part.shape[1]
    rows = mixed.shape[0]
    group = width // rows
    copies = []
    for h in range(kv_heads):
        values = jnp.concatenate([v[:, head_columns(h)] for v in value_refs], axis=0)
        rest = jnp.dot(last_weight[h], values, preferred_element_type=jnp.float32)
        for g in range(group):
            inside = slice(g * rows, (g + 1) * rows)
            columns = head_columns(h * group + g)
            mixed[:, columns] = (part[h, inside, :] + gate_row[:, columns] * rest[inside, :]).astype(jnp.bfloat16)
        columns = pl.ds(h * group * HEAD_SIZE, group * HEAD_SIZE)
        copies.append(pltpu.make_async_copy(mixed.at[:, columns], mixed_hbm.at[:, columns], sems.at[h]))
        copies[-1].start()
    for copy in copies:
        copy.wait()


def on_device(queries, keys, values, span_mask, section, section_gate):
    rows, wide = queries.shape
    heads, kv_heads = wide // HEAD_SIZE, keys.shape[1] // HEAD_SIZE
    width = heads // kv_heads * rows
    count = lax.axis_size("tm")
    per_span = CH // rows
    spans = count // per_span
    params = pltpu.CompilerParams(vmem_limit_bytes=24 * 1024 * 1024)
    acc_shape = jax.ShapeDtypeStruct((kv_heads, width, 2 * HEAD_SIZE), jnp.float32)

    def cost(blocks, times=3):
        return pl.CostEstimate(
            flops=4 * times * blocks * rows * rows * wide, bytes_accessed=rows * wide * 8, transcendentals=blocks * rows * rows * heads
        )

    cores = lax.axis_size("head")

    def send(value, target):
        pairs = []
        for i in range(count):
            for core in range(cores):
                if target(i) is None:
                    goal = i * cores + (core + 1) % cores if cores > 1 else i
                else:
                    goal = target(i) * cores + core
                pairs.append((i * cores + core, goal))
        return lax.ppermute(value, ("tm", "head"), pairs)

    def onward(value, distance):
        first = (distance - 1) * per_span

        def target(i):
            if i < first:
                return None
            return i + per_span if i + per_span < count else first + i % per_span

        return send(value, target)

    def around(value, distance, turn):
        return send(
            value, lambda i: i - i % per_span + (i + turn) % per_span if i >= distance * per_span else None
        )

    def leap(value):
        return send(value, lambda i: (i - per_span) % count)

    def travel(held, distance, far_values):
        onwards = [onward(x, distance + 1) for x in held] if distance + 1 < spans else []
        turned = [[around(x, distance, turn) for turn in range(1, per_span)] for x in (held if onwards else held[:1])]
        if not onwards:
            turned.append(far_values)
        return list(zip(*turned)), onwards

    floor = pl.pallas_call(
        floor_kernel,
        out_shape=jax.ShapeDtypeStruct((8, width), jnp.float32),
        out_specs=VMEM,
        compiler_params=params,
        cost_estimate=cost(4, 10),
        name="floor",
    )()
    held = [onward(x, 1) for x in (keys, values)] if spans > 1 else []
    near_keys, near_values, floor = lax.optimization_barrier((keys, values, floor))
    turned = list(zip(*[[around(x, 0, turn) for turn in range(1, per_span)] for x in (near_keys, near_values)]))
    def own(*refs):
        own_kernel(per_span, *refs)

    stacked, tails, gate_row, tops, acc = pl.pallas_call(
        own,
        out_shape=(
            jax.ShapeDtypeStruct((kv_heads, width, 2 * HEAD_SIZE), jnp.bfloat16),
            jax.ShapeDtypeStruct((spans, rows, HEAD_SIZE), jnp.bfloat16),
            jax.ShapeDtypeStruct((1, wide), jnp.float32),
            jax.ShapeDtypeStruct((heads, rows), jnp.float32),
            acc_shape,
        ),
        in_specs=[pl.BlockSpec(memory_space=pltpu.SMEM)] * 2 + [VMEM] * 2 + [HBM] * 3,
        out_specs=(VMEM,) * 5,
        scratch_shapes=[
            pltpu.VMEM(queries.shape, queries.dtype),
            pltpu.VMEM(keys.shape, keys.dtype),
            pltpu.VMEM(values.shape, values.dtype),
            pltpu.SemaphoreType.DMA((3,)),
        ],
        compiler_params=params,
        cost_estimate=cost(1, 5),
        name="own",
    )(span_mask, section, section_gate, floor, queries, keys, values)

    beside = [v for _, v in turned]
    far_values = [leap(v) for v in beside] if spans == 2 else None
    seen_blocks = [(0, (keys, values))]
    for distance in range(1, spans):
        waiting = [(distance - 1, t) for t in turned]
        forward = []
        for x in held:
            x, acc = lax.optimization_barrier((x, acc))
            forward.append(x)
        held = forward
        waiting.append((distance, tuple(held)))
        turned, held = travel(held, distance, far_values)
        distances = [d for d, _ in waiting]
        blocks = [k for _, (k, _) in waiting] + [v for _, (_, v) in waiting]
        seen_blocks += waiting

        def step(*refs, distances=distances):
            step_kernel(distances, *refs)

        acc = pl.pallas_call(
            step,
            out_shape=acc_shape,
            in_specs=[VMEM] * (3 + len(blocks)),
            out_specs=VMEM,
            compiler_params=params,
            cost_estimate=cost(len(waiting)),
            name="step_%d" % distance,
        )(stacked, tails, acc, *blocks)
        if far_values is None:
            far_values = []
            for x in beside:
                x, acc = lax.optimization_barrier((x, acc))
                far_values.append(leap(x))

    for i, (k, v) in enumerate(turned):
        v, acc = lax.optimization_barrier((v, acc))
        turned[i] = (k, v)
    distances = [d for d, _ in seen_blocks] + [spans - 1] * len(turned)

    def close(*refs):
        close_kernel(distances, len(turned), *refs)

    blocks = [k for _, (k, _) in seen_blocks] + [k for k, _ in turned] + [v for _, (_, v) in seen_blocks]
    part, last_weight, log_total = pl.pallas_call(
        close,
        out_shape=(
            jax.ShapeDtypeStruct((kv_heads, width, HEAD_SIZE), jnp.float32),
            jax.ShapeDtypeStruct((kv_heads, width, len(turned) * rows), jnp.bfloat16),
            jax.ShapeDtypeStruct((heads, rows), jnp.float32),
        ),
        in_specs=[VMEM] * (5 + len(blocks)),
        out_specs=(VMEM,) * 3,
        compiler_params=params,
        cost_estimate=cost(2),
        name="close",
    )(stacked, tails, gate_row, tops, acc, *blocks)
    mixed = pl.pallas_call(
        mix_kernel,
        out_shape=jax.ShapeDtypeStruct((rows, wide), jnp.bfloat16),
        in_specs=[VMEM] * (3 + len(turned)),
        out_specs=HBM,
        scratch_shapes=[pltpu.VMEM((rows, wide), jnp.bfloat16), pltpu.SemaphoreType.DMA((kv_heads,))],
        compiler_params=params,
        cost_estimate=cost(2),
        name="mix",
    )(gate_row, part, last_weight, *[v for _, v in turned])
    return mixed, log_total


def solution(mesh):
    placed = (
        P(("grp", "tm"), "head"),
        P(("grp", "tm"), "head"),
        P(("grp", "tm"), "head"),
        P("grp", None),
        P("grp"),
        P(None, "head"),
    )
    return jax.shard_map(
        on_device,
        mesh=mesh,
        in_specs=placed,
        out_specs=(P(("grp", "tm"), "head"), P("head", ("grp", "tm"))),
        check_vma=False,
    )
```

```python
import math

import jax
import jax.numpy as jnp
from jax import lax
from jax.experimental import pallas as pl
from jax.experimental.pallas import tpu as pltpu
from jax.sharding import PartitionSpec as P

HEAD_SIZE = 128
CH = 256
LOG2E = math.log2(math.e)
LN2 = math.log(2.0)
FAR = 1e30
SCALE = LOG2E / math.sqrt(HEAD_SIZE)
HBM = pl.BlockSpec(memory_space=pltpu.HBM)
VMEM = pl.BlockSpec(memory_space=pltpu.VMEM)


def head_columns(h):
    return slice(h * HEAD_SIZE, (h + 1) * HEAD_SIZE)


def scores_of(k, queries):
    return SCALE * lax.dot_general(k, queries, (((1,), (1,)), ((), ())), preferred_element_type=jnp.float32)


def times_values(v, weight):
    return lax.dot_general(v, weight, (((0,), (0,)), ((), ())), preferred_element_type=jnp.float32)


def floor_kernel(floor):
    floor[...] = jnp.full(floor.shape, -FAR, jnp.float32)


def own_kernel(floor, q_hbm, k_hbm, v_hbm, stacked, acc, stat, q, k, v, sems):
    copies = [
        pltpu.make_async_copy(src, dst, sems.at[i])
        for i, (src, dst) in enumerate([(q_hbm, q), (k_hbm, k), (v_hbm, v)])
    ]
    for copy in copies:
        copy.start()
    for copy in copies:
        copy.wait()
    rows = q.shape[0]
    group = stacked.shape[1] // rows
    for h in range(stacked.shape[0]):
        for g in range(group):
            stacked[h, g * rows : (g + 1) * rows, :] = q[:, head_columns(h * group + g)]
    for h in range(stacked.shape[0]):
        score = scores_of(k[:, head_columns(h)], stacked[h])
        top = jnp.maximum(floor[0:1, :], jnp.max(score, axis=0, keepdims=True))
        weight = jnp.exp2(score - top)
        stat[h, 0:1, :] = top
        stat[h, 1:2, :] = jnp.sum(weight, axis=0, keepdims=True)
        acc[h] = times_values(v[:, head_columns(h)], weight.astype(jnp.bfloat16))


def flag_kernel(per_span, mask, section, gate, seen, gate_row):
    span = lax.axis_index("tm") // per_span
    for distance in range(seen.shape[0]):
        allowed = jnp.logical_and(span >= distance, mask[span, jnp.maximum(span - distance, 0)] > 0)
        seen[distance : distance + 1, :] = jnp.full((1, seen.shape[1]), allowed.astype(jnp.int32), jnp.int32)
    gate_row[...] = gate[pl.ds(section[span], 1), :]


def weigh(h, distances, stacked, seen, stat, key_refs):
    scores = [scores_of(k[:, head_columns(h)], stacked[h]) for k in key_refs]
    flags = [seen[d : d + 1, :] > 0 for d in distances]
    old = stat[h, 0:1, :]
    top = old
    for score, flag in zip(scores, flags):
        top = jnp.maximum(top, jnp.where(flag, jnp.max(score, axis=0, keepdims=True), -FAR))
    weights = [jnp.exp2(score - jnp.where(flag, top, FAR)) for score, flag in zip(scores, flags)]
    factor = jnp.exp2(old - top)
    total = stat[h, 1:2, :] * factor
    for weight in weights:
        total += jnp.sum(weight, axis=0, keepdims=True)
    return weights, top, total, factor


def step_kernel(distances, stacked, seen, acc_in, stat_in, *refs):
    count = len(distances)
    key_refs, value_refs, (acc, stat) = refs[:count], refs[count : 2 * count], refs[2 * count :]
    for h in range(stacked.shape[0]):
        weights, top, total, factor = weigh(h, distances, stacked, seen, stat_in, key_refs)
        stat[h, 0:1, :] = top
        stat[h, 1:2, :] = total
        acc[h] = acc_in[h] * factor + times_values(
            jnp.concatenate([v[:, head_columns(h)] for v in value_refs], axis=0),
            jnp.concatenate([weight.astype(jnp.bfloat16) for weight in weights], axis=0),
        )


def close_kernel(distances, stacked, seen, gate_row, acc_in, stat_in, *refs):
    key_refs, (part, last_weight, log_ref) = refs[: len(distances)], refs[len(distances) :]
    rows = log_ref.shape[1]
    group = stacked.shape[1] // rows
    for h in range(stacked.shape[0]):
        weights, top, total, factor = weigh(h, distances, stacked, seen, stat_in, key_refs)
        inverse = 1.0 / total
        log_total = top * LN2 + jnp.log(total)
        turned = (acc_in[h] * (factor * inverse)).T
        for at, weight in enumerate(weights):
            last_weight[h, :, head_columns(at)] = (weight * inverse).T.astype(jnp.bfloat16)
        for g in range(group):
            head = h * group + g
            inside = slice(g * rows, (g + 1) * rows)
            part[h, inside, :] = turned[inside, :] * gate_row[:, head_columns(head)]
            log_ref[head : head + 1, :] = log_total[:, inside]


def mix_kernel(gate_row, part, last_weight, *refs):
    value_refs, (mixed_hbm, mixed, sems) = refs[:-3], refs[-3:]
    kv_heads, width = part.shape[0], part.shape[1]
    rows = mixed.shape[0]
    group = width // rows
    copies = []
    for h in range(kv_heads):
        values = jnp.concatenate([v[:, head_columns(h)] for v in value_refs], axis=0)
        rest = jnp.dot(last_weight[h], values, preferred_element_type=jnp.float32)
        for g in range(group):
            inside = slice(g * rows, (g + 1) * rows)
            columns = head_columns(h * group + g)
            mixed[:, columns] = (part[h, inside, :] + gate_row[:, columns] * rest[inside, :]).astype(jnp.bfloat16)
        columns = pl.ds(h * group * HEAD_SIZE, group * HEAD_SIZE)
        copies.append(pltpu.make_async_copy(mixed.at[:, columns], mixed_hbm.at[:, columns], sems.at[h]))
        copies[-1].start()
    for copy in copies:
        copy.wait()


def on_device(queries, keys, values, span_mask, section, section_gate):
    rows, wide = queries.shape
    heads, kv_heads = wide // HEAD_SIZE, keys.shape[1] // HEAD_SIZE
    width = heads // kv_heads * rows
    count = lax.axis_size("tm")
    per_span = CH // rows
    spans = count // per_span
    params = pltpu.CompilerParams(vmem_limit_bytes=24 * 1024 * 1024)
    acc_shape = jax.ShapeDtypeStruct((kv_heads, HEAD_SIZE, width), jnp.float32)
    stat_shape = jax.ShapeDtypeStruct((kv_heads, 8, width), jnp.float32)

    def cost(blocks, times=2):
        return pl.CostEstimate(
            flops=4 * times * blocks * rows * rows * wide, bytes_accessed=rows * wide * 8, transcendentals=blocks * rows * rows * heads
        )

    cores = lax.axis_size("head")

    def send(value, target):
        pairs = []
        for i in range(count):
            for core in range(cores):
                if target(i) is None:
                    goal = i * cores + (core + 1) % cores if cores > 1 else i
                else:
                    goal = target(i) * cores + core
                pairs.append((i * cores + core, goal))
        return lax.ppermute(value, ("tm", "head"), pairs)

    def onward(value, distance):
        first = (distance - 1) * per_span

        def target(i):
            if i < first:
                return None
            return i + per_span if i + per_span < count else first + i % per_span

        return send(value, target)

    def around(value, distance, turn):
        return send(
            value, lambda i: i - i % per_span + (i + turn) % per_span if i >= distance * per_span else None
        )

    def travel(held, distance, turned_before):
        onwards = [onward(x, distance + 1) for x in held] if distance + 1 < spans else []
        turned = [[around(x, distance, turn) for turn in range(1, per_span)] for x in held]
        if not onwards and turned_before:
            turned[1] = [onward(v, distance) for _, v in turned_before]
        return list(zip(*turned)), onwards

    floor = pl.pallas_call(
        floor_kernel,
        out_shape=jax.ShapeDtypeStruct((8, width), jnp.float32),
        out_specs=VMEM,
        compiler_params=params,
        cost_estimate=cost(4, 10),
        name="floor",
    )()
    held = [onward(x, 1) for x in (keys, values)] if spans > 1 else []
    near_keys, near_values, floor = lax.optimization_barrier((keys, values, floor))
    turned = list(zip(*[[around(x, 0, turn) for turn in range(1, per_span)] for x in (near_keys, near_values)]))
    def own(mask, section, gate, floor, q, k, v, seen, gate_row, *refs):
        flag_kernel(per_span, mask, section, gate, seen, gate_row)
        own_kernel(floor, q, k, v, *refs)

    seen, gate_row, stacked, acc, stat = pl.pallas_call(
        own,
        out_shape=(
            jax.ShapeDtypeStruct((spans, width), jnp.int32),
            jax.ShapeDtypeStruct((1, wide), jnp.float32),
            jax.ShapeDtypeStruct((kv_heads, width, HEAD_SIZE), jnp.bfloat16), acc_shape, stat_shape,
        ),
        in_specs=[pl.BlockSpec(memory_space=pltpu.SMEM)] * 2 + [VMEM] * 2 + [HBM] * 3,
        out_specs=(VMEM,) * 5,
        scratch_shapes=[
            pltpu.VMEM(queries.shape, queries.dtype),
            pltpu.VMEM(keys.shape, keys.dtype),
            pltpu.VMEM(values.shape, values.dtype),
            pltpu.SemaphoreType.DMA((3,)),
        ],
        compiler_params=params,
        cost_estimate=cost(1, 10),
        name="own",
    )(span_mask, section, section_gate, floor, queries, keys, values)
    for distance in range(1, spans):
        waiting = [(distance - 1, t) for t in turned] + [(distance, tuple(held))]
        forward = []
        for x in held:
            x, stat = lax.optimization_barrier((x, stat))
            forward.append(x)
        held = forward
        waiting[-1] = (distance, tuple(held))
        turned, held = travel(held, distance, turned)
        distances = [d for d, _ in waiting]

        count_in = 2 * len(waiting)
        blocks = [k for _, (k, _) in waiting] + [v for _, (_, v) in waiting]
        if True:

            def step(*refs, distances=distances):
                step_kernel(distances, *refs)

            acc, stat = pl.pallas_call(
                step,
                out_shape=(acc_shape, stat_shape),
                in_specs=[VMEM] * (4 + count_in),
                out_specs=(VMEM,) * 2,
                compiler_params=params,
                cost_estimate=cost(len(waiting)),
                name="step_%d" % distance,
            )(stacked, seen, acc, stat, *blocks)

    distances = [spans - 1] * len(turned)

    def close(*refs):
        close_kernel(distances, *refs)

    part, last_weight, log_total = pl.pallas_call(
        close,
        out_shape=(
            jax.ShapeDtypeStruct((kv_heads, width, HEAD_SIZE), jnp.float32),
            jax.ShapeDtypeStruct((kv_heads, width, len(turned) * rows), jnp.bfloat16),
            jax.ShapeDtypeStruct((heads, rows), jnp.float32),
        ),
        in_specs=[VMEM] * (5 + len(turned)),
        out_specs=(VMEM,) * 3,
        compiler_params=params,
        cost_estimate=cost(1),
        name="close",
    )(stacked, seen, gate_row, acc, stat, *[k for k, _ in turned])
    mixed = pl.pallas_call(
        mix_kernel,
        out_shape=jax.ShapeDtypeStruct((rows, wide), jnp.bfloat16),
        in_specs=[VMEM] * (3 + len(turned)),
        out_specs=HBM,
        scratch_shapes=[pltpu.VMEM((rows, wide), jnp.bfloat16), pltpu.SemaphoreType.DMA((kv_heads,))],
        compiler_params=params,
        cost_estimate=cost(1),
        name="mix",
    )(gate_row, part, last_weight, *[v for _, v in turned])
    return mixed, log_total


def solution(mesh):
    placed = (
        P(("grp", "tm"), "head"),
        P(("grp", "tm"), "head"),
        P(("grp", "tm"), "head"),
        P("grp", None),
        P("grp"),
        P(None, "head"),
    )
    return jax.shard_map(
        on_device,
        mesh=mesh,
        in_specs=placed,
        out_specs=(P(("grp", "tm"), "head"), P("head", ("grp", "tm"))),
        check_vma=False,
    )
```
